32 devices in a mesh: dp: 8 (over y, x, core), tensor: 4 (over z).
Axes of the slice: x: 2, y: 2, z: 4, core: 2. Of those that a mesh axis runs over, the one named last changes fastest.
Arguments:
- codes: int32 [16, 1024], P('dp'), may hold values from 0 to 1023
- doc_lengths: int32 [16, 3], P('dp'), may hold values from 1 to 896, 1024 in all within a row
- loss_mask: int32 [16, 1024], P('dp'), may hold values from 0 to 1
- qkv_master: float32 [1024, 3, 1024], P('dp', None, 'tensor'), may hold values from -0.1875 to 0.1875
- qkv_first: float32 [1024, 3, 1024], P('dp', None, 'tensor'), may hold values from -3.33786e-06 to 3.33786e-06
- qkv_second: float32 [1024, 3, 1024], P('dp', None, 'tensor'), may hold values from 2.7238338e-13 to 1.0895335e-12
- out_master: float32 [1024, 1024], P('tensor', 'dp'), may hold values from -1.5 to 1.5
- out_first: float32 [1024, 1024], P('tensor', 'dp'), may hold values from -3.33786e-06 to 3.33786e-06
- out_second: float32 [1024, 1024], P('tensor', 'dp'), may hold values from 2.7238338e-13 to 1.0895335e-12
- up_master: float32 [1024, 4096], P('dp', 'tensor'), may hold values from -0.1875 to 0.1875
- up_first: float32 [1024, 4096], P('dp', 'tensor'), may hold values from -3.33786e-06 to 3.33786e-06
- up_second: float32 [1024, 4096], P('dp', 'tensor'), may hold values from 2.7238338e-13 to 1.0895335e-12
- down_master: float32 [4096, 1024], P('tensor', 'dp'), may hold values from -0.09375 to 0.09375
- down_first: float32 [4096, 1024], P('tensor', 'dp'), may hold values from -3.33786e-06 to 3.33786e-06
- down_second: float32 [4096, 1024], P('tensor', 'dp'), may hold values from 2.7238338e-13 to 1.0895335e-12
- table_master: float32 [2, 1025, 1024], P(None, None, ('dp', 'tensor')), may hold values from -0.375 to 0.375
- table_first: float32 [2, 1025, 1024], P(None, None, ('dp', 'tensor')), may hold values from -3.33786e-06 to 3.33786e-06
- table_second: float32 [2, 1025, 1024], P(None, None, ('dp', 'tensor')), may hold values from 2.7238338e-13 to 1.0895335e-12
- gain_master: float32 [3, 1024], P(None, ('dp', 'tensor')), may hold values from 0.3 to 2.1, as said below
- gain_first: float32 [3, 1024], P(None, ('dp', 'tensor')), may hold values from -3.0517578e-05 to 3.0517578e-05
- gain_second: float32 [3, 1024], P(None, ('dp', 'tensor')), may hold values from 2.7238338e-11 to 1.0895335e-10
Outputs:
- qkv_new: float32 [1024, 3, 1024], P('dp', None, 'tensor')
- qkv_first_new: float32 [1024, 3, 1024], P('dp', None, 'tensor')
- qkv_second_new: float32 [1024, 3, 1024], P('dp', None, 'tensor')
- qkv_copy: bfloat16 [1024, 3, 1024], P('dp', None, 'tensor')
- out_new: float32 [1024, 1024], P('tensor', 'dp')
- out_first_new: float32 [1024, 1024], P('tensor', 'dp')
- out_second_new: float32 [1024, 1024], P('tensor', 'dp')
- out_copy: bfloat16 [1024, 1024], P('tensor', 'dp')
- up_new: float32 [1024, 4096], P('dp', 'tensor')
- up_first_new: float32 [1024, 4096], P('dp', 'tensor')
- up_second_new: float32 [1024, 4096], P('dp', 'tensor')
- up_copy: bfloat16 [1024, 4096], P('dp', 'tensor')
- down_new: float32 [4096, 1024], P('tensor', 'dp')
- down_first_new: float32 [4096, 1024], P('tensor', 'dp')
- down_second_new: float32 [4096, 1024], P('tensor', 'dp')
- down_copy: bfloat16 [4096, 1024], P('tensor', 'dp')
- table_new: float32 [2, 1025, 1024], P(None, None, ('dp', 'tensor'))
- table_first_new: float32 [2, 1025, 1024], P(None, None, ('dp', 'tensor'))
- table_second_new: float32 [2, 1025, 1024], P(None, None, ('dp', 'tensor'))
- table_copy: bfloat16 [2, 1025, 1024], P(None, None, ('dp', 'tensor'))
- gain_new: float32 [3, 1024], P(None, ('dp', 'tensor'))
- gain_first_new: float32 [3, 1024], P(None, ('dp', 'tensor'))
- gain_second_new: float32 [3, 1024], P(None, ('dp', 'tensor'))
- gain_copy: bfloat16 [3, 1024], P(None, ('dp', 'tensor'))
- loss_total: float32 [], replicated
- count_total: float32 [], replicated
- grad_norm: float32 [], replicated
The draws below stay inside these ranges and needn't reach their ends.
Inputs may be any that keep to these rules, and one draw needn't show every extreme that they name: `gain_master`: positive gains.
All inputs are finite; a program needn't handle non-finite values.
Results may differ from the reference program's by a relative error of at most 0.0086.
Values may be sent and summed in bfloat16 or wider, within the bound.
No kernel may reach another device: no remote copies, remote signals or barrier semaphores. Data moves between devices by JAX's collectives and lax.ppermute only.
A program may use at most 192 MiB of HBM per device.

```python
import math
import jax
import jax.numpy as jnp
import numpy as np
from jax import lax

D = 1024
HEADS = 16
HEAD = 64
FF = 4096
VOCAB = 1025
PACK = 1024
STEP = 5
PACKS = 16


def draw_gain_master(key, part):
    key = jax.random.fold_in(key, 3)
    rising = 0.5 + jnp.arange(D).astype(jnp.float32) / D
    spread = jax.random.uniform(key, (3, D), jnp.float32, 0.8, 1.2)
    return spread * rising[None, :]


def draw_loss_mask(key, part):
    key = jax.random.fold_in(key, 5)
    row_level = 450 * jnp.arange(PACKS, dtype=jnp.int32) // PACKS
    col_level = 450 * jnp.arange(PACK, dtype=jnp.int32) // PACK
    level = 50 + row_level[:, None] + col_level[None, :]
    rolled = jax.random.randint(key, (PACKS, PACK), 0, 1000, dtype=jnp.int32)
    return (rolled < level).astype(jnp.int32)


def with_ends(drawn, key, least, top_value):
    index_at = [jax.random.randint(jax.random.fold_in(key, axis), (), 0, length) for axis, length in enumerate(drawn.shape)]
    main_axis = drawn.shape.index(max(drawn.shape))
    neighbour = index_at[:main_axis] + [(index_at[main_axis] + 1) % drawn.shape[main_axis]] + index_at[main_axis + 1:]
    return drawn.at[tuple(index_at)].set(least).at[tuple(neighbour)].set(top_value)


def steps_of(rng, dims, shards, least, top_value):
    def one(dim, shards_of):
        steps = jax.random.uniform(jax.random.fold_in(jax.random.fold_in(rng, 6), dim), (shards_of,), jnp.float32, least / len(shards), top_value / len(shards))
        return jnp.repeat(jnp.exp(steps), dims[dim] // shards_of).reshape((-1,) + (1,) * (len(dims) - dim - 1))

    factor_of = one(*shards[0])
    for cut in shards[1:]:
        factor_of = factor_of * one(*cut)
    return factor_of


def split_up(number_of, total, limit, skew):
    loads = [(1 << 20) // math.isqrt(standing ** skew) + 1 for standing in range(2, number_of + 1)]
    rest, given = total - limit - (number_of - 1), [1] * (number_of - 1)
    while rest > 0:
        free = [i for i in range(number_of - 1) if given[i] < limit]
        pool, budget = sum([loads[i] for i in free]), rest
        for i in free:
            addition = min(limit - given[i], max(1, budget * loads[i] // pool), rest)
            given[i] = given[i] + addition
            rest = rest - addition
    return np.array([limit] + given)


def ragged(stream_key, amount, total, bound, lean):
    if amount == 2:
        one = jax.random.randint(stream_key, (), max(1, total - bound), min(bound, total - 1) + 1)
        return jnp.stack([one, total - one])
    lengths = jnp.asarray(split_up(amount, total, bound, lean), jnp.int32)
    twos = (amount - 1) // 2
    source_of, taker = lengths[1:1 + 2 * twos:2], lengths[2:2 + 2 * twos:2]
    room = jnp.minimum(source_of - 1, bound - taker)
    shifted = jax.random.randint(jax.random.fold_in(stream_key, 1), (twos,), 0, 1 << 20) % (room + 1)
    lengths = lengths.at[1:1 + 2 * twos:2].set(source_of - shifted).at[2:2 + 2 * twos:2].set(taker + shifted)
    return lengths[jax.random.permutation(jax.random.fold_in(stream_key, 2), amount)]


def normal_values(stream_key, dims, scale, reach, pieces=(), held_as=jnp.bfloat16):
    gain = steps_of(stream_key, dims, pieces, -0.22, 0.18) if pieces else 1.0
    entries = jax.random.normal(stream_key, dims, jnp.float32) * scale * gain
    return jnp.minimum(jnp.maximum(entries, -reach), reach).astype(held_as)


def setup_inputs(seed: int = 0) -> dict:
    key_list = jax.random.split(jax.random.key(seed), 22)
    codes = with_ends(jax.random.randint(key_list[0], (PACKS, PACK), 0, VOCAB - 1), jax.random.fold_in(key_list[0], 1), 0, (VOCAB - 1) - 1).astype(jnp.int32)
    doc_lengths = jax.vmap(lambda own: ragged(own, 3, PACK, PACK - PACK // 8, 2))(jax.random.split(key_list[1], PACKS)).reshape((PACKS, 3)).astype(jnp.int32)
    loss_mask = draw_loss_mask(jax.random.fold_in(key_list[21], 71), 0)
    qkv_master = normal_values(key_list[3], (D, 3, D), D ** -0.5, 0.1875, ((0, 8), (2, 4)), jnp.float32)
    qkv_first = normal_values(key_list[4], (D, 3, D), (0.002 * (4 * D * D + 2 * D * FF + 2 * VOCAB * D + 3 * D) ** -0.5), 3.337860107421875e-06, ((0, 8), (2, 4)), jnp.float32)
    qkv_second = jnp.clip(jnp.exp(math.log(1.0895335198282674e-12) - 1.3862944 * jax.random.uniform(key_list[5], (D, 3, D), jnp.float32) ** steps_of(key_list[5], (D, 3, D), ((0, 8), (2, 4)), -0.2, 0.2)), 2.7238337995706685e-13, 1.0895335198282674e-12)
    out_master = normal_values(key_list[6], (D, D), (D // 64) ** -0.5, 1.5, ((0, 4), (1, 8)), jnp.float32)
    out_first = normal_values(key_list[7], (D, D), (0.002 * (4 * D * D + 2 * D * FF + 2 * VOCAB * D + 3 * D) ** -0.5), 3.337860107421875e-06, ((0, 4), (1, 8)), jnp.float32)
    out_second = jnp.clip(jnp.exp(math.log(1.0895335198282674e-12) - 1.3862944 * jax.random.uniform(key_list[8], (D, D), jnp.float32) ** steps_of(key_list[8], (D, D), ((0, 4), (1, 8)), -0.2, 0.2)), 2.7238337995706685e-13, 1.0895335198282674e-12)
    up_master = normal_values(key_list[9], (D, FF), D ** -0.5, 0.1875, ((0, 8), (1, 4)), jnp.float32)
    up_first = normal_values(key_list[10], (D, FF), (0.002 * (4 * D * D + 2 * D * FF + 2 * VOCAB * D + 3 * D) ** -0.5), 3.337860107421875e-06, ((0, 8), (1, 4)), jnp.float32)
    up_second = jnp.clip(jnp.exp(math.log(1.0895335198282674e-12) - 1.3862944 * jax.random.uniform(key_list[11], (D, FF), jnp.float32) ** steps_of(key_list[11], (D, FF), ((0, 8), (1, 4)), -0.2, 0.2)), 2.7238337995706685e-13, 1.0895335198282674e-12)
    down_master = normal_values(key_list[12], (FF, D), FF ** -0.5, 0.09375, ((0, 4), (1, 8)), jnp.float32)
    down_first = normal_values(key_list[13], (FF, D), (0.002 * (4 * D * D + 2 * D * FF + 2 * VOCAB * D + 3 * D) ** -0.5), 3.337860107421875e-06, ((0, 4), (1, 8)), jnp.float32)
    down_second = jnp.clip(jnp.exp(math.log(1.0895335198282674e-12) - 1.3862944 * jax.random.uniform(key_list[14], (FF, D), jnp.float32) ** steps_of(key_list[14], (FF, D), ((0, 4), (1, 8)), -0.2, 0.2)), 2.7238337995706685e-13, 1.0895335198282674e-12)
    table_master = normal_values(key_list[15], (2, VOCAB, D), 0.06, 0.375, ((2, 32),), jnp.float32)
    table_first = normal_values(key_list[16], (2, VOCAB, D), (0.002 * (4 * D * D + 2 * D * FF + 2 * VOCAB * D + 3 * D) ** -0.5), 3.337860107421875e-06, ((2, 32),), jnp.float32)
    table_second = jnp.clip(jnp.exp(math.log(1.0895335198282674e-12) - 1.3862944 * jax.random.uniform(key_list[17], (2, VOCAB, D), jnp.float32) ** steps_of(key_list[17], (2, VOCAB, D), ((2, 32),), -0.2, 0.2)), 2.7238337995706685e-13, 1.0895335198282674e-12)
    gain_master = draw_gain_master(jax.random.fold_in(key_list[21], 71), 0)
    gain_first = normal_values(key_list[19], (3, D), (0.02 * (4 * D * D + 2 * D * FF + 2 * VOCAB * D + 3 * D) ** -0.5), 3.0517578125e-05, ((1, 32),), jnp.float32)
    gain_second = jnp.clip(jnp.exp(math.log(1.0895335328386935e-10) - 1.3862944 * jax.random.uniform(key_list[20], (3, D), jnp.float32) ** steps_of(key_list[20], (3, D), ((1, 32),), -0.2, 0.2)), 2.7238338320967337e-11, 1.0895335328386935e-10)
    return dict(codes=codes, doc_lengths=doc_lengths, loss_mask=loss_mask, qkv_master=qkv_master, qkv_first=qkv_first, qkv_second=qkv_second, out_master=out_master, out_first=out_first, out_second=out_second, up_master=up_master, up_first=up_first, up_second=up_second, down_master=down_master, down_first=down_first, down_second=down_second, table_master=table_master, table_first=table_first, table_second=table_second, gain_master=gain_master, gain_first=gain_first, gain_second=gain_second)


@jax.custom_vjp
def low(v):
    return lax.optimization_barrier(v.astype(jnp.bfloat16)).astype(jnp.float32)

@jax.custom_vjp
def low_back(v):
    return v

def low_keep(v):
    return (low(v), None)

def low_pass(kept, grad):
    return (grad,)

def back_keep(v):
    return (v, None)

def back_low(kept, grad):
    return (low(grad),)
low.defvjp(low_keep, low_pass)
low_back.defvjp(back_keep, back_low)
RATE_MATRIX = 0.03
RATE_GAIN = 0.25
DECAY_RATE = 0.01
CLIP_NORM = 0.002
NORM_EPS = 1e-05
ADAM_EPS = 1e-08
HIGHEST = lax.Precision.HIGHEST

def layer_norm(values, gain_vec):
    mean_val = lax.optimization_barrier(jnp.mean(values, -1, keepdims=True))
    centered = values - mean_val
    inverse = lax.rsqrt(lax.optimization_barrier(jnp.mean(centered * centered, -1, keepdims=True)) + NORM_EPS)
    return centered * inverse * gain_vec

def doc_layout(lengths_row, total_rows):
    places = jnp.arange(total_rows, dtype=jnp.int32)
    bound_one = lengths_row[0]
    bound_two = lengths_row[0] + lengths_row[1]
    doc_ids = (places >= bound_one).astype(jnp.int32) + (places >= bound_two).astype(jnp.int32)
    starts = jnp.where(doc_ids == 0, 0, jnp.where(doc_ids == 1, bound_one, bound_two))
    return (doc_ids, places - starts)

def next_codes(codes_row, doc_ids, end_code):
    later = jnp.concatenate([codes_row[1:], jnp.full((1,), end_code, jnp.int32)])
    later_doc = jnp.concatenate([doc_ids[1:], jnp.full((1,), -1, jnp.int32)])
    return jnp.where(later_doc == doc_ids, later, end_code).astype(jnp.int32)

def position_code(local_pos, width):
    halves = jnp.arange(width // 2).astype(jnp.float32)
    freqs = jnp.exp(halves * (-2.0 * math.log(10000.0) / width))
    angles = local_pos.astype(jnp.float32)[:, None] * freqs[None, :]
    return jnp.stack([jnp.sin(angles), jnp.cos(angles)], -1).reshape(local_pos.shape[0], width)

def allowed_block(doc_ids, first_row, block_rows):
    total_rows = doc_ids.shape[0]
    row_pos = first_row + jnp.arange(block_rows, dtype=jnp.int32)
    col_pos = jnp.arange(total_rows, dtype=jnp.int32)
    row_doc = lax.dynamic_slice_in_dim(doc_ids, first_row, block_rows, 0)
    return (col_pos[None, :] <= row_pos[:, None]) & (doc_ids[None, :] == row_doc[:, None])

def pack_loss(params, codes_row, lengths_row, mask_row):
    qkv_w, out_w, up_w, down_w, table_w, gain_w = params
    total_rows = codes_row.shape[0]
    doc_ids, local_pos = doc_layout(lengths_row, total_rows)
    targets = next_codes(codes_row, doc_ids, VOCAB - 1)
    start = table_w[0][codes_row] * math.sqrt(D) + position_code(local_pos, D)
    attn_in = low(layer_norm(start, gain_w[0]))
    joined = low(low_back(jnp.dot(attn_in, qkv_w.reshape(D, 3 * D), precision=HIGHEST)))
    joined = joined.reshape(total_rows, 3, HEADS, HEAD)
    query = joined[:, 0]
    keys = joined[:, 1]
    values = joined[:, 2]
    block_rows = min(512, total_rows)

    def one_block(block_index):
        first_row = block_index * block_rows
        q_block = lax.dynamic_slice_in_dim(query, first_row, block_rows, 0)
        scores = low_back(jnp.einsum('bhe,khe->hbk', q_block, keys, precision=HIGHEST) * HEAD ** (-0.5))
        scores = jnp.where(allowed_block(doc_ids, first_row, block_rows)[None], scores, -1e+30)
        probs = low(jax.nn.softmax(scores, -1))
        return jnp.einsum('hbk,khe->bhe', probs, values, precision=HIGHEST)
    mixed = lax.map(jax.checkpoint(one_block), jnp.arange(total_rows // block_rows, dtype=jnp.int32))
    mixed = low(low_back(mixed.reshape(total_rows, D)))
    middle = start + low_back(jnp.dot(mixed, out_w, precision=HIGHEST))
    ffn_in = low(layer_norm(middle, gain_w[1]))
    up_val = low_back(jnp.dot(ffn_in, up_w, precision=HIGHEST))
    hidden = low(jax.nn.gelu(up_val, approximate=False))
    final = middle + low_back(jnp.dot(hidden, down_w, precision=HIGHEST))
    features = low(layer_norm(final, gain_w[2]))
    logits = low_back(lax.dot_general(features, table_w[1], (((1,), (1,)), ((), ())), precision=HIGHEST))
    picked = jnp.take_along_axis(logits, targets[:, None], 1)[:, 0]
    return jnp.sum(mask_row.astype(jnp.float32) * (jax.nn.logsumexp(logits, -1) - picked))

def adam_update(master, first, second, grad, step_rate, decay_rate):
    first_new = 0.5 * first + 0.5 * grad
    second_new = 0.5 * second + 0.5 * grad * grad
    correct = 1.0 - 0.5 ** STEP
    master_new = master - step_rate * (first_new / correct / (jnp.sqrt(second_new / correct) + ADAM_EPS) + decay_rate * master)
    return (master_new, first_new, second_new, master_new.astype(jnp.bfloat16))

def reference(codes, doc_lengths, loss_mask, qkv_master, qkv_first, qkv_second, out_master, out_first, out_second, up_master, up_first, up_second, down_master, down_first, down_second, table_master, table_first, table_second, gain_master, gain_first, gain_second):
    masters = (qkv_master, out_master, up_master, down_master, table_master, gain_master)
    firsts = (qkv_first, out_first, up_first, down_first, table_first, gain_first)
    seconds = (qkv_second, out_second, up_second, down_second, table_second, gain_second)
    weights = tuple((m.astype(jnp.bfloat16).astype(jnp.float32) for m in masters))

    def total_loss(params):

        def one_pack(carry, packed):
            return (carry + jax.checkpoint(pack_loss)(params, packed[0], packed[1], packed[2]), None)
        result, _ = lax.scan(one_pack, jnp.zeros((), jnp.float32), (codes, doc_lengths, loss_mask))
        return result
    loss_sum, pull_back = jax.vjp(total_loss, weights)
    grads = pull_back(jnp.ones((), jnp.float32))[0]
    count_all = jnp.sum(loss_mask.astype(jnp.float32))
    reduced = tuple((g / count_all for g in grads))
    norm_all = jnp.sqrt(sum((jnp.sum(g * g) for g in reduced)))
    factor = jnp.minimum(1.0, CLIP_NORM / (norm_all + 1e-06))
    q_new, q_first, q_second, q_copy = adam_update(masters[0], firsts[0], seconds[0], reduced[0] * factor, RATE_MATRIX, DECAY_RATE)
    o_new, o_first, o_second, o_copy = adam_update(masters[1], firsts[1], seconds[1], reduced[1] * factor, RATE_MATRIX, DECAY_RATE)
    u_new, u_first, u_second, u_copy = adam_update(masters[2], firsts[2], seconds[2], reduced[2] * factor, RATE_MATRIX, DECAY_RATE)
    d_new, d_first, d_second, d_copy = adam_update(masters[3], firsts[3], seconds[3], reduced[3] * factor, RATE_MATRIX, DECAY_RATE)
    t_new, t_first, t_second, t_copy = adam_update(masters[4], firsts[4], seconds[4], reduced[4] * factor, RATE_MATRIX, DECAY_RATE)
    g_new, g_first, g_second, g_copy = adam_update(masters[5], firsts[5], seconds[5], reduced[5] * factor, RATE_GAIN, 0.0)
    return (q_new, q_first, q_second, q_copy, o_new, o_first, o_second, o_copy, u_new, u_first, u_second, u_copy, d_new, d_first, d_second, d_copy, t_new, t_first, t_second, t_copy, g_new, g_first, g_second, g_copy, loss_sum, count_all, norm_all)
```

```python
import functools
import math

import jax
import jax.numpy as jnp
from jax import lax
from jax.experimental import pallas as pl
from jax.experimental.pallas import tpu as pltpu
from jax.sharding import PartitionSpec as P

HEAD = 64
STEP = 5

RATE_MATRIX = 0.03
RATE_GAIN = 0.25
DECAY_RATE = 0.01
CLIP_NORM = 0.002
NORM_EPS = 1e-05
ADAM_EPS = 1e-08

BF = jnp.bfloat16
F32 = jnp.float32
LOG2E = math.log2(math.e)
NN = (((1,), (0,)), ((), ()))
NT = (((1,), (1,)), ((), ()))
TN = (((0,), (0,)), ((), ()))
VMEM_BYTES = 48 * 1024 * 1024


def dot(left, right, dims=NN):
    return lax.dot_general(left, right, dims, preferred_element_type=F32)


def barrier(*values):
    return lax.optimization_barrier(values)


class Place:
    def __init__(self):
        self.dp = lax.axis_size("dp")
        self.nz = lax.axis_size("tensor")
        self.ny = self.dp // 4
        index = lax.axis_index("dp")
        self.z = lax.axis_index("tensor")
        self.c = index % 2
        self.x = (index // 2) % 2
        self.y = index // 4
        self.blocks = [(0, 0), (0, 1)]
        self.blocks += [(k, 1) for k in range(1, self.ny)]
        self.blocks += [(k, 0) for k in range(1, self.ny)]

    def at(self, ky, kx):
        return self.blocks.index((ky, kx))

    def swap_c(self, value):
        return lax.ppermute(value, "dp", [(i, i ^ 1) for i in range(self.dp)])

    def swap_x(self, value):
        return lax.ppermute(value, "dp", [(i, i ^ 2) for i in range(self.dp)])

    def from_y(self, value, k):
        n = self.dp
        return lax.ppermute(value, "dp", [((i + 4 * k) % n, i) for i in range(n)])

    def to_y(self, value, k):
        n = self.dp
        return lax.ppermute(value, "dp", [(i, (i + 4 * k) % n) for i in range(n)])

    def from_z(self, value, k):
        n = self.nz
        return lax.ppermute(value, "tensor", [((i + k) % n, i) for i in range(n)])

    def to_z(self, value, k):
        n = self.nz
        return lax.ppermute(value, "tensor", [(i, (i + k) % n) for i in range(n)])

    def total(self, value):
        value = value + self.swap_c(value)
        value = value + self.swap_x(value)
        value = value + sum(self.from_y(value, k) for k in range(1, self.ny))
        return value + sum(self.from_z(value, k) for k in range(1, self.nz))

    def in_order(self, mine, other, axis):
        first = jnp.where(self.c == 0, mine, other)
        last = jnp.where(self.c == 0, other, mine)
        return jnp.concatenate([first, last], axis)


def gather_z(place, piece):
    return [piece] + [place.from_z(piece, k) for k in range(1, place.nz)]


def join_z(parts, axis):
    half = len(parts) // 2
    return jnp.stack([jnp.concatenate(parts[:half], axis), jnp.concatenate(parts[half:], axis)])


def gather_xy_one(place, both):
    return place.swap_x(both), [place.from_y(both, k) for k in range(1, place.ny)]


def gather_xy_two(place, by_x, by_y):
    first = [place.swap_x(v[0]) for v in by_y]
    second = [place.from_y(by_x[1], k) for k in range(1, place.ny)]
    return first, second


def gathered(place, both, by_x, by_y, far_a, far_b):
    out = []
    for half, far in ((0, far_a), (1, far_b)):
        out.append([both[half], by_x[half]] + far + [v[half] for v in by_y])
    return out


def sum_xy_one(place, send_a, send_b):
    return place.swap_x(send_a), [place.to_y(v, k + 1) for k, v in enumerate(send_b)]


def sum_xy_two(place, pass_a, pass_b):
    return [place.to_y(v, k + 1) for k, v in enumerate(pass_a)], place.swap_x(pass_b)


def forward_kernel(c_ref, start_ref, qkv_ref, o_ref, lse_ref, k_s, v_s):
    c = c_ref[0]
    half = qkv_ref.shape[1]
    total = 2 * half
    block = min(256, half)
    per_half = half // block
    scale = HEAD ** (-0.5) * LOG2E
    for b in range(2):
        k_s[b * half : (b + 1) * half] = qkv_ref[b ^ c, :, 128:256]
        v_s[b * half : (b + 1) * half] = qkv_ref[b ^ c, :, 256:384]
    lane = lax.broadcasted_iota(jnp.int32, (block, 128), 1)
    for qb in range(total // block):
        rel = (qb // per_half) ^ c
        r0 = (qb % per_half) * block
        n = (qb + 1) * block
        q = qkv_ref[rel, r0 : r0 + block, 0:128]
        row = qb * block + lax.broadcasted_iota(jnp.int32, (block, n), 0)
        col = lax.broadcasted_iota(jnp.int32, (block, n), 1)
        start = start_ref[qb * block : (qb + 1) * block, 0:1]
        allowed = (col >= start) & (col <= row)
        outs = []
        for h in range(2):
            qh = jnp.where((lane >= 64) == (h == 1), q, jnp.zeros_like(q))
            s = dot(qh, k_s[0:n], NT)
            s = jnp.where(allowed, s, -1e30)
            top = jnp.max(s, -1, keepdims=True)
            p = jnp.exp2((s - top) * scale)
            total_p = jnp.sum(p, -1, keepdims=True)
            outs.append(dot(p.astype(BF), v_s[0:n]) / total_p)
            lse = top * scale + jnp.log2(total_p)
            lse_ref[0, qb * block : (qb + 1) * block, h * 64 : (h + 1) * 64] = jnp.broadcast_to(
                lse, (block, 64)
            )
        o_ref[rel, r0 : r0 + block, :] = jnp.where(lane < 64, outs[0], outs[1]).astype(BF)


def backward_kernel(c_ref, start_ref, qkv_ref, o_ref, go_ref, lse_ref, out_ref, k_s, v_s, gk_s, gv_s):
    c = c_ref[0]
    half = qkv_ref.shape[1]
    total = 2 * half
    block = min(256, half)
    per_half = half // block
    scale = HEAD ** (-0.5)
    for b in range(2):
        k_s[b * half : (b + 1) * half] = qkv_ref[b ^ c, :, 128:256]
        v_s[b * half : (b + 1) * half] = qkv_ref[b ^ c, :, 256:384]
    lane = lax.broadcasted_iota(jnp.int32, (block, 128), 1)
    for step, qb in enumerate(reversed(range(total // block))):
        rel = (qb // per_half) ^ c
        r0 = (qb % per_half) * block
        n = (qb + 1) * block
        q = qkv_ref[rel, r0 : r0 + block, 0:128]
        go = go_ref[rel, r0 : r0 + block, :]
        o = o_ref[rel, r0 : r0 + block, :]
        row = qb * block + lax.broadcasted_iota(jnp.int32, (block, n), 0)
        col = lax.broadcasted_iota(jnp.int32, (block, n), 1)
        start = start_ref[qb * block : (qb + 1) * block, 0:1]
        allowed = (col >= start) & (col <= row)
        both = go.astype(F32) * o.astype(F32)
        gq = None
        for h in range(2):
            mine = (lane >= 64) == (h == 1)
            qh = jnp.where(mine, q, jnp.zeros_like(q))
            gh = jnp.where(mine, go, jnp.zeros_like(go))
            s = dot(qh, k_s[0:n], NT)
            lse = lse_ref[0, qb * block : (qb + 1) * block, h * 64 : h * 64 + 1]
            p = jnp.where(allowed, jnp.exp2(jnp.minimum(s * (scale * LOG2E) - lse, 1.0)), 0.0)
            gp = dot(gh, v_s[0:n], NT)
            inner = jnp.sum(jnp.where(mine, both, 0.0), -1, keepdims=True)
            gs = (p * (gp - inner)).astype(BF)
            pb = p.astype(BF)
            gqh = dot(gs, k_s[0:n])
            gq = gqh if gq is None else jnp.where(lane < 64, gq, gqh)
            gk = dot(gs, qh, TN)
            gv = dot(pb, gh, TN)
            if step == 0 and h == 0:
                gk_s[0:n] = gk
                gv_s[0:n] = gv
            else:
                gk_s[0:n] += gk
                gv_s[0:n] += gv
        out_ref[rel, r0 : r0 + block, 0:128] = (gq * scale).astype(BF)
    for b in range(2):
        out_ref[b ^ c, :, 128:256] = (gk_s[b * half : (b + 1) * half] * scale).astype(BF)
        out_ref[b ^ c, :, 256:384] = gv_s[b * half : (b + 1) * half].astype(BF)


def attention(c_index, starts, qkv):
    rows, cols = qkv.shape
    half, pairs = rows // 2, cols // 384
    smem = pl.BlockSpec(memory_space=pltpu.SMEM)
    out, lse = pl.pallas_call(
        forward_kernel,
        grid=(pairs,),
        in_specs=[
            smem,
            pl.BlockSpec((rows, 1), lambda j: (0, 0)),
            pl.BlockSpec((2, half, 384), lambda j: (0, 0, j)),
        ],
        out_specs=[
            pl.BlockSpec((2, half, 128), lambda j: (0, 0, j)),
            pl.BlockSpec((1, rows, 128), lambda j: (j, 0, 0)),
        ],
        out_shape=[
            jax.ShapeDtypeStruct((2, half, pairs * 128), BF),
            jax.ShapeDtypeStruct((pairs, rows, 128), F32),
        ],
        scratch_shapes=[pltpu.VMEM((rows, 128), BF), pltpu.VMEM((rows, 128), BF)],
        compiler_params=pltpu.CompilerParams(vmem_limit_bytes=VMEM_BYTES),
        cost_estimate=pl.CostEstimate(
            flops=4 * pairs * 2 * rows * rows * 128, bytes_accessed=2 * rows * cols * 3, transcendentals=0
        ),
        name="attend",
    )(c_index, starts, qkv.reshape(2, half, cols))
    return out.reshape(rows, pairs * 128), lse


def attention_back(c_index, starts, qkv, out, grad, lse):
    rows, cols = qkv.shape
    half, pairs = rows // 2, cols // 384
    smem = pl.BlockSpec(memory_space=pltpu.SMEM)
    wide = pl.BlockSpec((2, half, 384), lambda j: (0, 0, j))
    thin = pl.BlockSpec((2, half, 128), lambda j: (0, 0, j))
    result = pl.pallas_call(
        backward_kernel,
        grid=(pairs,),
        in_specs=[
            smem,
            pl.BlockSpec((rows, 1), lambda j: (0, 0)),
            wide,
            thin,
            thin,
            pl.BlockSpec((1, rows, 128), lambda j: (j, 0, 0)),
        ],
        out_specs=wide,
        out_shape=jax.ShapeDtypeStruct((2, half, cols), BF),
        scratch_shapes=[
            pltpu.VMEM((rows, 128), BF),
            pltpu.VMEM((rows, 128), BF),
            pltpu.VMEM((rows, 128), F32),
            pltpu.VMEM((rows, 128), F32),
        ],
        compiler_params=pltpu.CompilerParams(vmem_limit_bytes=VMEM_BYTES),
        cost_estimate=pl.CostEstimate(
            flops=10 * pairs * 2 * rows * rows * 128, bytes_accessed=2 * rows * cols * 4, transcendentals=0
        ),
        name="attend_back",
    )(
        c_index,
        starts,
        qkv.reshape(2, half, cols),
        out.reshape(2, half, pairs * 128),
        grad.reshape(2, half, pairs * 128),
        lse,
    )
    return result.reshape(rows, cols)


def layer_norm(values, gain_vec):
    mean_val = jnp.mean(values, -1, keepdims=True)
    centered = values - mean_val
    inverse = lax.rsqrt(jnp.mean(centered * centered, -1, keepdims=True) + NORM_EPS)
    normed = centered * inverse
    return ((normed * gain_vec).astype(BF), normed, inverse)


def norm_back(grad_out, normed, inverse, gain_vec):
    grad_normed = grad_out * gain_vec
    grad_in = inverse * (
        grad_normed
        - jnp.mean(grad_normed, -1, keepdims=True)
        - normed * jnp.mean(grad_normed * normed, -1, keepdims=True)
    )
    return (grad_in, jnp.sum(grad_out * normed, 0))


def doc_layout(lengths_row, total_rows):
    places = jnp.arange(total_rows, dtype=jnp.int32)
    bound_one = lengths_row[0]
    bound_two = lengths_row[0] + lengths_row[1]
    doc_ids = (places >= bound_one).astype(jnp.int32) + (places >= bound_two).astype(jnp.int32)
    starts = jnp.where(doc_ids == 0, 0, jnp.where(doc_ids == 1, bound_one, bound_two))
    return (doc_ids, starts, places - starts)


def next_codes(codes_row, doc_ids, end_code):
    later = jnp.concatenate([codes_row[1:], jnp.full((1,), end_code, jnp.int32)])
    later_doc = jnp.concatenate([doc_ids[1:], jnp.full((1,), -1, jnp.int32)])
    return jnp.where(later_doc == doc_ids, later, end_code)


def head_loss(logits, targets, weights_row):
    top_score = jnp.max(logits, -1, keepdims=True)
    expo = jnp.exp(logits - top_score)
    totals = jnp.sum(expo, -1, keepdims=True)
    target_hit = jnp.arange(logits.shape[1], dtype=jnp.int32)[None, :] == targets[:, None]
    picked = jnp.sum(jnp.where(target_hit, logits, 0.0), -1)
    loss_value = jnp.sum(weights_row * (top_score[:, 0] + jnp.log(totals[:, 0]) - picked))
    grad_logits = ((expo / totals - target_hit.astype(F32)) * weights_row[:, None]).astype(BF)
    return (loss_value, grad_logits)


def adam_update(master, first, second, grad, step_rate, decay_rate):
    first_new = 0.5 * first + 0.5 * grad
    second_new = 0.5 * second + 0.5 * grad * grad
    correct = 1.0 - 0.5**STEP
    master_new = master - step_rate * (
        first_new / correct / (jnp.sqrt(second_new / correct) + ADAM_EPS) + decay_rate * master
    )
    return (master_new, first_new, second_new, master_new.astype(BF))


def gelu_both(value):
    phi = 0.5 * (1.0 + lax.erf(value * (0.5**0.5)))
    slope = phi + value * (jnp.exp(-0.5 * value * value) * (1.0 / math.sqrt(2.0 * math.pi)))
    return (value * phi).astype(BF), slope.astype(BF)


def body(
    codes,
    doc_lengths,
    loss_mask,
    qkv_master,
    qkv_first,
    qkv_second,
    out_master,
    out_first,
    out_second,
    up_master,
    up_first,
    up_second,
    down_master,
    down_first,
    down_second,
    table_master,
    table_first,
    table_second,
    gain_master,
    gain_first,
    gain_second,
):
    place = Place()
    nz, ny, nb = place.nz, place.ny, len(place.blocks)
    c, z = place.c, place.z
    feat = qkv_master.shape[0]
    width = feat * place.dp
    total_rows = codes.shape[1]
    half_rows = total_rows // 2
    vocab = table_master.shape[1]
    thin = table_master.shape[2]

    joined = jnp.concatenate([codes, loss_mask, doc_lengths], 1)
    other = place.swap_c(joined)
    four = place.in_order(joined, other, 0)
    row = lax.dynamic_index_in_dim(four, z, 0, keepdims=False)
    codes_row = row[:total_rows]
    mask_row = row[total_rows : 2 * total_rows]
    lengths_row = row[2 * total_rows :]
    doc_ids, starts, local_pos = doc_layout(lengths_row, total_rows)
    targets = next_codes(codes_row, doc_ids, vocab - 1)
    first_row = c * half_rows
    my_codes = lax.dynamic_slice_in_dim(codes_row, first_row, half_rows, 0)
    my_local = lax.dynamic_slice_in_dim(local_pos, first_row, half_rows, 0)
    my_targets = lax.dynamic_slice_in_dim(targets, first_row, half_rows, 0)
    my_mask = lax.dynamic_slice_in_dim(mask_row, first_row, half_rows, 0).astype(F32)
    c_index = jnp.reshape(c, (1,)).astype(jnp.int32)
    starts_col = starts.reshape(total_rows, 1)

    def halves(matrix, axis):
        size = matrix.shape[axis] // 2
        keep = lax.dynamic_slice_in_dim(matrix, c * size, size, axis)
        send = lax.dynamic_slice_in_dim(matrix, (1 - c) * size, size, axis)
        return keep, send

    qkv_b, out_b, up_b, down_b = (
        v.astype(BF) for v in (qkv_master, out_master, up_master, down_master)
    )
    qkv_k, qkv_s = (v.reshape(feat, -1) for v in halves(qkv_b, 2))
    out_k, out_s = (v.T for v in halves(out_b, 0))
    up_k, up_s = halves(up_b, 1)
    down_k, down_s = (v.T for v in halves(down_b, 0))
    units = [v.shape[1] for v in (qkv_k, out_k, up_k, down_k)]
    keep = jnp.concatenate([qkv_k, out_k, up_k, down_k], 1)
    send = jnp.concatenate([qkv_s, out_s, up_s, down_s], 1)
    table_t = jnp.swapaxes(table_master.astype(BF), 1, 2)
    embed_p = jnp.concatenate([table_t[0], gain_master.astype(BF).T], 1)
    head_p = table_t[1]

    recv = place.swap_c(send)
    chip = place.in_order(keep, recv, 0)
    edges = [sum(units[:i]) for i in range(5)]
    qkv_p, out_p, up_p, down_p = (chip[:, edges[i] : edges[i + 1]] for i in range(4))

    pieces = [(embed_p, 0), (qkv_p, 1), (out_p, 1), (up_p, 1), (down_p, 1), (head_p, 0)]
    plan = [
        [("z", 0), ("z", 1)],
        [("one", 0), ("one", 1), ("z", 2), ("z", 3)],
        [("two", 0), ("two", 1), ("one", 2), ("one", 3)],
        [("two", 2), ("two", 3), ("z", 4), ("z", 5)],
        [("one", 4), ("one", 5)],
        [("two", 4), ("two", 5)],
    ]
    stage = [dict(own=v[0]) for v in pieces]
    full = {}
    for slot in plan:
        live = [s for i, s in enumerate(stage) if i not in full]
        order = [i for i in range(len(stage)) if i not in full]
        (live,) = barrier(live)
        for i, s in zip(order, live):
            stage[i] = dict(s)
        for kind, i in slot:
            s = stage[i]
            if kind == "z":
                s["parts"] = gather_z(place, s["own"])
            elif kind == "one":
                s["both"] = join_z(s["parts"], pieces[i][1])
                s["by_x"], s["by_y"] = gather_xy_one(place, s["both"])
            else:
                s["far_a"], s["far_b"] = gather_xy_two(place, s["by_x"], s["by_y"])
        (stage_out,) = barrier([stage[i] for i in order])
        for i, s in zip(order, stage_out):
            stage[i] = dict(s)
        for kind, i in slot:
            if kind == "two":
                s = stage[i]
                full[i] = gathered(
                    place, s["both"], s["by_x"], s["by_y"], s["far_a"], s["far_b"]
                )

    def weight(i):
        return [jnp.concatenate(v, 0) for v in full[i]]

    def table(i):
        a, b = (jnp.stack(v) for v in full[i])
        cols = a.shape[-1]
        rel = jnp.concatenate([a, b], 1).reshape(nb, nz, thin, cols)
        mine = jnp.roll(rel, z, 1).reshape(nb, 1, nz * thin, cols)
        got = place.swap_c(mine)
        return place.in_order(mine, got, 1).reshape(width, cols)

    embed_t = table(0)
    gains = embed_t[:, vocab:].astype(F32).T
    wqkv, wout, wup, wdown = weight(1), weight(2), weight(3), weight(4)
    head_t = table(5)

    block = jnp.asarray([k for k, _ in place.blocks], jnp.int32)
    block_x = jnp.asarray([k for _, k in place.blocks], jnp.int32)
    chip_at = ((place.y + block) % ny) * 2 + (place.x ^ block_x)
    feature = (
        chip_at[:, None] * (2 * feat) + jnp.arange(2 * feat, dtype=jnp.int32)[None, :]
    ).reshape(width)
    freqs = jnp.exp((feature // 2).astype(F32) * (-2.0 * math.log(10000.0) / width))
    angles = my_local.astype(F32)[:, None] * freqs[None, :]
    coded = jnp.where((feature % 2 == 0)[None, :], jnp.sin(angles), jnp.cos(angles))
    one_hot = (
        my_codes[:, None] == jnp.arange(embed_t.shape[1], dtype=jnp.int32)[None, :]
    ).astype(BF)
    start = dot(one_hot, embed_t, NT) * math.sqrt(width) + coded
    attn_m, normed_one, inverse_one = layer_norm(start, gains[0])

    def pair(mine):
        return jnp.concatenate([mine, place.swap_c(mine)], 0)

    def branch(lefts, rights, dims):
        theirs = sum(dot(v[half_rows:], w, dims) for v, w in zip(lefts, rights)).astype(BF)
        got = place.swap_c(theirs)
        mine = sum(dot(v[:half_rows], w, dims) for v, w in zip(lefts, rights))
        return mine + got.astype(F32)

    attn_in = pair(attn_m)
    qkv = [dot(attn_in, w).astype(BF) for w in wqkv]
    mixed, lse = [], []
    for v in qkv:
        o, ls = attention(c_index, starts_col, v)
        mixed.append(o)
        lse.append(ls)
    middle = start + branch(mixed, wout, NT)
    ffn_m, normed_two, inverse_two = layer_norm(middle, gains[1])
    ffn_in = pair(ffn_m)
    hidden, slope = zip(*(gelu_both(dot(ffn_in, w)) for w in wup))
    final = middle + branch(hidden, wdown, NT)
    features, normed_three, inverse_three = layer_norm(final, gains[2])
    logits = dot(features, head_t)
    loss_local, grad_logits = head_loss(logits, my_targets, my_mask)

    cut = 2 * feat

    def weight_grad(left, rights):
        def piece(lo, hi, right):
            return dot(left[:, lo * cut : hi * cut], right, TN)

        a, b = rights
        send_a = piece(1, 1 + ny, a).astype(BF)
        if ny == 2:
            send_b = [piece(2, 4, b).astype(BF)]
        else:
            send_b = [
                jnp.concatenate(
                    [piece(place.at(k, 1), place.at(k, 1) + 1, b), piece(place.at(k, 0), place.at(k, 0) + 1, b)]
                ).astype(BF)
                for k in range(1, ny)
            ]
        got_a, got_b = sum_xy_one(place, send_a, send_b)
        pass_a = [
            (piece(place.at(k, 0), place.at(k, 0) + 1, a) + got_a[k * cut : (k + 1) * cut].astype(F32)).astype(BF)
            for k in range(1, ny)
        ]
        pass_b = (piece(1, 2, b) + sum(v[:cut].astype(F32) for v in got_b)).astype(BF)
        far_a, far_b = sum_xy_two(place, pass_a, pass_b)
        own_a = piece(0, 1, a) + got_a[:cut].astype(F32) + sum(v.astype(F32) for v in far_a)
        own_b = piece(0, 1, b) + sum(v[cut:].astype(F32) for v in got_b) + far_b.astype(F32)
        return own_a, own_b

    def sum_z(own_a, own_b, axis):
        chunks = jnp.split(own_a, nz // 2, axis) + jnp.split(own_b, nz // 2, axis)
        return chunks[0] + sum(
            place.to_z(chunks[k].astype(BF), k).astype(F32) for k in range(1, nz)
        )

    def table_grad(partial):
        cols = partial.shape[1]
        cut_t = partial.reshape(nb, 2, nz * thin, cols)
        keep_t = lax.dynamic_index_in_dim(cut_t, c, 1, keepdims=False)
        send_t = lax.dynamic_index_in_dim(cut_t, 1 - c, 1, keepdims=False)
        chip_t = keep_t.astype(F32) + place.swap_c(send_t.astype(BF)).astype(F32)
        rel = jnp.roll(chip_t.reshape(nb, nz, thin, cols), -z, 1)
        a = rel[:, : nz // 2]
        b = rel[:, nz // 2 :]
        send_a = a[1 : 1 + ny].astype(BF)
        send_b = [
            jnp.stack([b[place.at(k, 1)], b[place.at(k, 0)]]).astype(BF) for k in range(1, ny)
        ]
        got_a, got_b = sum_xy_one(place, send_a, send_b)
        pass_a = [(a[place.at(k, 0)] + got_a[k].astype(F32)).astype(BF) for k in range(1, ny)]
        pass_b = (b[1] + sum(v[0].astype(F32) for v in got_b)).astype(BF)
        far_a, far_b = sum_xy_two(place, pass_a, pass_b)
        own_a = a[0] + got_a[0].astype(F32) + sum(v.astype(F32) for v in far_a)
        own_b = b[0] + sum(v[1].astype(F32) for v in got_b) + far_b.astype(F32)
        return sum_z(own_a, own_b, 0)[0]

    head_grad = dot(features, grad_logits, TN)
    head_sum = table_grad(head_grad)
    grad_feat = dot(grad_logits, head_t, NT)
    grad_final, gain_three = norm_back(grad_feat, normed_three, inverse_three, gains[2])
    grad_down = pair(grad_final.astype(BF))
    down_own = weight_grad(grad_down, hidden)
    grad_up = [(dot(grad_down, w) * s.astype(F32)).astype(BF) for w, s in zip(wdown, slope)]
    up_own = weight_grad(ffn_in, grad_up)
    grad_mid, gain_two = norm_back(branch(grad_up, wup, NT), normed_two, inverse_two, gains[1])
    grad_mid = grad_mid + grad_final
    grad_out = pair(grad_mid.astype(BF))
    out_own = weight_grad(grad_out, mixed)
    grad_mixed = [dot(grad_out, w).astype(BF) for w in wout]
    grad_qkv = [
        attention_back(c_index, starts_col, q, o, g, ls)
        for q, o, g, ls in zip(qkv, mixed, grad_mixed, lse)
    ]
    qkv_own = weight_grad(attn_in, grad_qkv)
    grad_start, gain_one = norm_back(
        branch(grad_qkv, wqkv, NT), normed_one, inverse_one, gains[0]
    )
    grad_start = grad_start + grad_mid
    embed_grad = dot((grad_start * math.sqrt(width)).astype(BF), one_hot[:, :vocab], TN)
    gain_grad = jnp.stack([gain_one, gain_two, gain_three], 1)
    embed_sum = table_grad(jnp.concatenate([embed_grad, gain_grad], 1))

    sums = jnp.concatenate(
        [sum_z(*v, 1) for v in (qkv_own, out_own, up_own, down_own)], 1
    )
    keep_g, send_g = halves(sums, 0)
    got_g = place.swap_c(send_g)
    chunks_k = [keep_g[:, edges[i] : edges[i + 1]] for i in range(4)]
    chunks_g = [got_g[:, edges[i] : edges[i + 1]] for i in range(4)]
    qkv_g = place.in_order(
        chunks_k[0].reshape(feat, 3, -1), chunks_g[0].reshape(feat, 3, -1), 2
    )
    out_g = place.in_order(chunks_k[1].T, chunks_g[1].T, 0)
    up_g = place.in_order(chunks_k[2], chunks_g[2], 1)
    down_g = place.in_order(chunks_k[3].T, chunks_g[3].T, 0)
    table_g = jnp.stack([embed_sum[:, :vocab].T, head_sum.T])
    gain_g = embed_sum[:, vocab:].T
    summed = (qkv_g, out_g, up_g, down_g, table_g, gain_g)

    stats = place.total(jnp.stack([loss_local, jnp.sum(my_mask)]))
    loss_all, count_all = stats[0], stats[1]
    squares = (
        jnp.sum(sums * sums) + jnp.sum(embed_sum * embed_sum) + jnp.sum(head_sum * head_sum)
    )
    square_all = place.total(squares.reshape(1))[0] / (count_all * count_all)
    norm_all = jnp.sqrt(square_all)
    factor = jnp.minimum(1.0, CLIP_NORM / (norm_all + 1e-06))
    masters = (qkv_master, out_master, up_master, down_master, table_master, gain_master)
    firsts = (qkv_first, out_first, up_first, down_first, table_first, gain_first)
    seconds = (qkv_second, out_second, up_second, down_second, table_second, gain_second)
    results = []
    for i in range(6):
        step_rate = RATE_GAIN if i == 5 else RATE_MATRIX
        decay_rate = 0.0 if i == 5 else DECAY_RATE
        clipped = summed[i] / count_all * factor
        results.extend(
            adam_update(masters[i], firsts[i], seconds[i], clipped, step_rate, decay_rate)
        )
    return tuple(results) + (loss_all, count_all, norm_all)


def solution(mesh):
    rows, cols = P("dp", None, "tensor"), P("tensor", "dp")
    plain, both, gain = P("dp", "tensor"), P(None, None, ("dp", "tensor")), P(None, ("dp", "tensor"))
    kinds = (rows, cols, plain, cols, both, gain)
    in_specs = (P("dp", None),) * 3 + tuple(k for k in kinds for _ in range(3))
    out_specs = tuple(k for k in kinds for _ in range(4)) + (P(),) * 3
    return jax.shard_map(body, mesh=mesh, in_specs=in_specs, out_specs=out_specs, check_vma=False)
```

```python
import functools
import math

import jax
import jax.numpy as jnp
from jax import lax
from jax.experimental import pallas as pl
from jax.experimental.pallas import tpu as pltpu
from jax.sharding import PartitionSpec as P

HEAD = 64
STEP = 5

RATE_MATRIX = 0.03
RATE_GAIN = 0.25
DECAY_RATE = 0.01
CLIP_NORM = 0.002
NORM_EPS = 1e-05
ADAM_EPS = 1e-08

BF = jnp.bfloat16
F32 = jnp.float32
LOG2E = math.log2(math.e)
NN = (((1,), (0,)), ((), ()))
NT = (((1,), (1,)), ((), ()))
TN = (((0,), (0,)), ((), ()))
VMEM_BYTES = 28 * 1024 * 1024
SMALL_VMEM = 24 * 1024 * 1024


def dot(left, right, dims=NN):
    return lax.dot_general(left, right, dims, preferred_element_type=F32)


def barrier(*values):
    return lax.optimization_barrier(values)


class Place:
    def __init__(self):
        self.dp = lax.axis_size("dp")
        self.nz = lax.axis_size("tensor")
        self.ny = self.dp // 4
        index = lax.axis_index("dp")
        self.z = lax.axis_index("tensor")
        self.c = index % 2
        self.x = (index // 2) % 2
        self.y = index // 4
        self.blocks = [(0, 0), (0, 1)]
        self.blocks += [(k, 1) for k in range(1, self.ny)]
        self.blocks += [(k, 0) for k in range(1, self.ny)]

    def at(self, ky, kx):
        return self.blocks.index((ky, kx))

    def swap_c(self, value):
        return lax.ppermute(value, "dp", [(i, i ^ 1) for i in range(self.dp)])

    def swap_x(self, value):
        return lax.ppermute(value, "dp", [(i, i ^ 2) for i in range(self.dp)])

    def from_y(self, value, k):
        n = self.dp
        return lax.ppermute(value, "dp", [((i + 4 * k) % n, i) for i in range(n)])

    def to_y(self, value, k):
        n = self.dp
        return lax.ppermute(value, "dp", [(i, (i + 4 * k) % n) for i in range(n)])

    def from_z(self, value, k):
        n = self.nz
        return lax.ppermute(value, "tensor", [((i + k) % n, i) for i in range(n)])

    def to_z(self, value, k):
        n = self.nz
        return lax.ppermute(value, "tensor", [(i, (i + k) % n) for i in range(n)])

    def all_z(self, value):
        return lax.all_to_all(value, "tensor", 0, 0)

    def total(self, value):
        value = value + self.swap_c(value)
        n = self.dp
        around = [
            lax.ppermute(value, "dp", [(((i ^ (2 * kx)) + 4 * ky) % n, i) for i in range(n)])
            for ky, kx in self.blocks[1:]
        ]
        value = value + sum(around)
        return value + sum(self.from_z(value, k) for k in range(1, self.nz))

    def in_order(self, mine, other, axis):
        first = jnp.where(self.c == 0, mine, other)
        last = jnp.where(self.c == 0, other, mine)
        return jnp.concatenate([first, last], axis)


class Cell:
    def __init__(self, value):
        self.v = value


def cells(*values):
    return [Cell(v) for v in values]


def fence(*held):
    held = list(dict.fromkeys(held))
    for cell, value in zip(held, barrier(*[c.v for c in held])):
        cell.v = value


class Slots:
    def __init__(self):
        self.flight = []

    def slot(self, stages, *also, wait=True):
        plans = [stage() for stage in stages]
        sends = [s for plan, _ in plans for s in plan]
        fence(*(self.flight if wait else ()), *[c for _, c in sends], *also)
        out = [Cell(send(c.v)) for send, c in sends]
        self.flight = out if wait else self.flight + out
        at = 0
        for plan, take in plans:
            take(out[at : at + len(plan)])
            at += len(plan)


class Gather:
    def __init__(self, place, own, axis, groups=None):
        self.place, self.own, self.axis, self.groups = place, Cell(own), axis, groups
        self.ks = range(1, place.ny)

    def over_z(self, *after):
        place = self.place
        fence(self.own, *after)
        own = self.own.v
        self.parts = Cell(place.all_z(jnp.broadcast_to(own[None], (place.nz,) + own.shape)))

    def near(self):
        place, half = self.place, self.place.nz // 2
        parts, groups = self.parts.v, self.groups or [(0, self.own.v.shape[1])]
        self.both = Cell(
            jnp.stack(
                [
                    jnp.concatenate(
                        [parts[i][:, g0:g1] for g0, g1 in groups for i in range(lo, lo + half)],
                        self.axis,
                    )
                    for lo in (0, half)
                ]
            )
        )

        def take(out):
            self.by_x, self.by_y = out[0], out[1:]

        plan = [(place.swap_x, self.both)]
        return plan + [(functools.partial(place.from_y, k=k), self.both) for k in self.ks], take

    def far(self):
        place = self.place

        def take(out):
            self.far_a, self.far_b = out[: place.ny - 1], out[place.ny - 1 :]

        plan = [(lambda v: place.swap_x(v[0]), v) for v in self.by_y]
        return plan + [(lambda v, k=k: place.from_y(v[1], k), self.by_x) for k in self.ks], take

    def pieces(self):
        out = []
        for half, far in ((0, self.far_a), (1, self.far_b)):
            out.append(
                [self.both.v[half], self.by_x.v[half]]
                + [v.v for v in far]
                + [v.v[half] for v in self.by_y]
            )
        return out

    def arrays(self):
        cells = [self.both, self.by_x, *self.far_a, *self.far_b, *self.by_y]
        return [c.v for c in cells]


class Reduce:
    def __init__(self, place, whole, axis, groups=None):
        self.place, self.whole, self.axis, self.groups = place, whole, axis, groups
        self.ks = range(1, place.ny)

    def near(self):
        place = self.place
        a, b = self.whole

        def take(out):
            self.got_a, self.got_b = out[0], out[1:]

        plan = [(place.swap_x, Cell(a[1 : 1 + place.ny]))]
        for k in self.ks:
            if place.ny == 2:
                sent = b[2:4]
            else:
                sent = jnp.stack([b[place.at(k, 1)], b[place.at(k, 0)]])
            plan.append((functools.partial(place.to_y, k=k), Cell(sent)))
        return plan, take

    def far(self):
        place = self.place
        a, b = self.whole

        def take(out):
            self.far_a, self.far_b = out[:-1], out[-1]

        def along(got, k):
            sent = a[place.at(k, 0)].astype(F32) + got[k].astype(F32)
            return place.to_y(sent.astype(BF), k)

        def across(first):
            sent = b[1].astype(F32) + first[0].astype(F32)
            for other in self.got_b[1:]:
                sent = sent + other.v[0].astype(F32)
            return place.swap_x(sent.astype(BF))

        plan = [(functools.partial(along, k=k), self.got_a) for k in self.ks]
        return plan + [(across, self.got_b[0])], take

    def over_z(self, *after):
        place, half = self.place, self.place.nz // 2
        a, b = self.whole
        own_a = a[0].astype(F32) + self.got_a.v[0].astype(F32) + sum(v.v.astype(F32) for v in self.far_a)
        own_b = (
            b[0].astype(F32) + sum(v.v[1].astype(F32) for v in self.got_b) + self.far_b.v.astype(F32)
        )
        if self.axis == 0:
            chunks = jnp.split(own_a, half, 0) + jnp.split(own_b, half, 0)
        else:
            chunks = []
            for own in (own_a, own_b):
                parts = [jnp.split(own[:, half * g0 : half * g1], half, 1) for g0, g1 in self.groups]
                chunks += [jnp.concatenate(v, 1) for v in zip(*parts)]
        sent = Cell(jnp.stack([v.astype(BF) for v in chunks]))
        fence(sent, *after)
        if self.axis == 0:
            pieces = [
                lax.dynamic_index_in_dim(sent.v, (place.z + k) % place.nz, 0, keepdims=False)
                for k in range(place.nz)
            ]
            moved = [place.to_z(pieces[k], k) for k in range(1, place.nz)]
            self.got = Cell(jnp.stack(pieces[:1] + moved))
        else:
            self.got = Cell(place.all_z(sent.v))

    def result(self):
        return jnp.sum(self.got.v.astype(F32), 0)


def forward_kernel(c_ref, start_ref, qkv_ref, o_ref, lse_ref, k_s, v_s):
    c = c_ref[0]
    half = qkv_ref.shape[1]
    total = 2 * half
    block = min(256, half)
    per_half = half // block
    scale = HEAD ** (-0.5) * LOG2E
    for b in range(2):
        k_s[b * half : (b + 1) * half] = qkv_ref[b ^ c, :, 128:256]
        v_s[b * half : (b + 1) * half] = qkv_ref[b ^ c, :, 256:384]
    lane = lax.broadcasted_iota(jnp.int32, (block, 128), 1)
    for qb in range(total // block):
        rel = (qb // per_half) ^ c
        r0 = (qb % per_half) * block
        n = (qb + 1) * block
        q = qkv_ref[rel, r0 : r0 + block, 0:128]
        row = qb * block + lax.broadcasted_iota(jnp.int32, (block, n), 0)
        col = lax.broadcasted_iota(jnp.int32, (block, n), 1)
        start = start_ref[qb * block : (qb + 1) * block, 0:1]
        allowed = (col >= start) & (col <= row)
        outs = []
        for h in range(2):
            qh = jnp.where((lane >= 64) == (h == 1), q, jnp.zeros_like(q))
            s = dot(qh, k_s[0:n], NT)
            s = jnp.where(allowed, s, -1e30)
            top = jnp.max(s, -1, keepdims=True)
            p = jnp.exp2((s - top) * scale)
            total_p = jnp.sum(p, -1, keepdims=True)
            outs.append(dot(p.astype(BF), v_s[0:n]) / total_p)
            lse = top * scale + jnp.log2(total_p)
            lse_ref[0, qb * block : (qb + 1) * block, h * 64 : (h + 1) * 64] = jnp.broadcast_to(
                lse, (block, 64)
            )
        o_ref[rel, r0 : r0 + block, :] = jnp.where(lane < 64, outs[0], outs[1]).astype(BF)


def backward_kernel(c_ref, start_ref, qkv_ref, o_ref, go_ref, lse_ref, out_ref, k_s, v_s, gk_s, gv_s):
    c = c_ref[0]
    half = qkv_ref.shape[1]
    total = 2 * half
    block = min(256, half)
    per_half = half // block
    scale = HEAD ** (-0.5)
    for b in range(2):
        k_s[b * half : (b + 1) * half] = qkv_ref[b ^ c, :, 128:256]
        v_s[b * half : (b + 1) * half] = qkv_ref[b ^ c, :, 256:384]
    lane = lax.broadcasted_iota(jnp.int32, (block, 128), 1)
    for step, qb in enumerate(reversed(range(total // block))):
        rel = (qb // per_half) ^ c
        r0 = (qb % per_half) * block
        n = (qb + 1) * block
        q = qkv_ref[rel, r0 : r0 + block, 0:128]
        go = go_ref[rel, r0 : r0 + block, :]
        o = o_ref[rel, r0 : r0 + block, :]
        row = qb * block + lax.broadcasted_iota(jnp.int32, (block, n), 0)
        col = lax.broadcasted_iota(jnp.int32, (block, n), 1)
        start = start_ref[qb * block : (qb + 1) * block, 0:1]
        allowed = (col >= start) & (col <= row)
        both = go.astype(F32) * o.astype(F32)
        gq = None
        for h in range(2):
            mine = (lane >= 64) == (h == 1)
            qh = jnp.where(mine, q, jnp.zeros_like(q))
            gh = jnp.where(mine, go, jnp.zeros_like(go))
            s = dot(qh, k_s[0:n], NT)
            lse = lse_ref[0, qb * block : (qb + 1) * block, h * 64 : h * 64 + 1]
            p = jnp.where(allowed, jnp.exp2(jnp.minimum(s * (scale * LOG2E) - lse, 1.0)), 0.0)
            gp = dot(gh, v_s[0:n], NT)
            inner = jnp.sum(jnp.where(mine, both, 0.0), -1, keepdims=True)
            gs = (p * (gp - inner)).astype(BF)
            pb = p.astype(BF)
            gqh = dot(gs, k_s[0:n])
            gq = gqh if gq is None else jnp.where(lane < 64, gq, gqh)
            gk = dot(gs, qh, TN)
            gv = dot(pb, gh, TN)
            if step == 0 and h == 0:
                gk_s[0:n] = gk
                gv_s[0:n] = gv
            else:
                gk_s[0:n] += gk
                gv_s[0:n] += gv
        out_ref[rel, r0 : r0 + block, 0:128] = (gq * scale).astype(BF)
    for b in range(2):
        out_ref[b ^ c, :, 128:256] = (gk_s[b * half : (b + 1) * half] * scale).astype(BF)
        out_ref[b ^ c, :, 256:384] = gv_s[b * half : (b + 1) * half].astype(BF)


def attention(c_index, starts, qkv):
    rows, cols = qkv.shape
    half, pairs = rows // 2, cols // 384
    smem = pl.BlockSpec(memory_space=pltpu.SMEM)
    out, lse = pl.pallas_call(
        forward_kernel,
        grid=(pairs,),
        in_specs=[
            smem,
            pl.BlockSpec((rows, 1), lambda j: (0, 0)),
            pl.BlockSpec((2, half, 384), lambda j: (0, 0, j)),
        ],
        out_specs=[
            pl.BlockSpec((2, half, 128), lambda j: (0, 0, j)),
            pl.BlockSpec((1, rows, 128), lambda j: (j, 0, 0)),
        ],
        out_shape=[
            jax.ShapeDtypeStruct((2, half, pairs * 128), BF),
            jax.ShapeDtypeStruct((pairs, rows, 128), F32),
        ],
        scratch_shapes=[pltpu.VMEM((rows, 128), BF), pltpu.VMEM((rows, 128), BF)],
        compiler_params=pltpu.CompilerParams(vmem_limit_bytes=VMEM_BYTES),
        cost_estimate=pl.CostEstimate(
            flops=1, bytes_accessed=1, transcendentals=0
        ),
        name="attend",
    )(c_index, starts, qkv.reshape(2, half, cols))
    return out.reshape(rows, pairs * 128), lse


def attention_back(c_index, starts, qkv, out, grad, lse):
    rows, cols = qkv.shape
    half, pairs = rows // 2, cols // 384
    smem = pl.BlockSpec(memory_space=pltpu.SMEM)
    wide = pl.BlockSpec((2, half, 384), lambda j: (0, 0, j))
    thin = pl.BlockSpec((2, half, 128), lambda j: (0, 0, j))
    result = pl.pallas_call(
        backward_kernel,
        grid=(pairs,),
        in_specs=[
            smem,
            pl.BlockSpec((rows, 1), lambda j: (0, 0)),
            wide,
            thin,
            thin,
            pl.BlockSpec((1, rows, 128), lambda j: (j, 0, 0)),
        ],
        out_specs=wide,
        out_shape=jax.ShapeDtypeStruct((2, half, cols), BF),
        scratch_shapes=[
            pltpu.VMEM((rows, 128), BF),
            pltpu.VMEM((rows, 128), BF),
            pltpu.VMEM((rows, 128), F32),
            pltpu.VMEM((rows, 128), F32),
        ],
        compiler_params=pltpu.CompilerParams(vmem_limit_bytes=VMEM_BYTES),
        cost_estimate=pl.CostEstimate(
            flops=1, bytes_accessed=1, transcendentals=0
        ),
        name="attend_back",
    )(
        c_index,
        starts,
        qkv.reshape(2, half, cols),
        out.reshape(2, half, pairs * 128),
        grad.reshape(2, half, pairs * 128),
        lse,
    )
    return result.reshape(rows, cols)


def cheap():
    return pl.CostEstimate(flops=1, bytes_accessed=1, transcendentals=0)


def call(kernel, args, shapes, scratch=(), name=None):
    vmem = pl.BlockSpec(memory_space=pltpu.VMEM)
    return pl.pallas_call(
        kernel,
        in_specs=[vmem] * len(args),
        out_specs=[vmem] * len(shapes),
        out_shape=shapes,
        scratch_shapes=list(scratch),
        compiler_params=pltpu.CompilerParams(vmem_limit_bytes=SMALL_VMEM),
        cost_estimate=cheap(),
        name=name,
    )(*args)


def piece_at(refs, blocks, half, i):
    far = (blocks - 2) // 2
    if i < 2:
        return refs[i].at[half]
    if i < 2 + far:
        return refs[i + half * far]
    return refs[i + far].at[half]


def gelu_parts(value):
    phi = 0.5 * (1.0 + lax.erf(value * (0.5**0.5)))
    slope = phi + value * (jnp.exp(-0.5 * value * value) * (1.0 / math.sqrt(2.0 * math.pi)))
    return value * phi, slope


def across_kernel(blocks, count, lo, hi, kind, *refs):
    mine_ref, theirs_ref = refs[:2]
    weights = refs[2 : 2 + count]
    refs = refs[2 + count :]
    slopes = ()
    if kind == "slope":
        slopes, refs = refs[:2], refs[2:]
    joined_ref, refs = refs[0], refs[1:]
    outs, w_s = refs[:-1], refs[-1]
    rows = mine_ref.shape[0]
    tile = min(512, rows)
    size = w_s.shape[1] // blocks
    for half in range(2):
        for i in range(blocks):
            w_s[half, i * size : (i + 1) * size] = piece_at(weights, blocks, half, i)[:, lo:hi]
    for base, source in ((0, mine_ref), (rows, theirs_ref)):

        @pl.loop(0, rows // tile)
        def _(step):
            r = pl.multiple_of(step * tile, tile)
            at = pl.ds(pl.multiple_of(base + step * tile, tile), tile)
            left = source[pl.ds(r, tile), :]
            joined_ref[at, :] = left
            for half in range(2):
                value = dot(left, w_s[half])
                if kind == "gelu":
                    value, slope = gelu_parts(value)
                    outs[2 + half][at, :] = slope.astype(BF)
                elif kind == "slope":
                    value = value * slopes[half][at, :].astype(F32)
                outs[half][at, :] = value.astype(BF)


def across(mine, theirs, gather, span, kind="plain", slopes=()):
    arrays = gather.arrays()
    blocks = len(gather.place.blocks)
    lo, hi = span
    rows, width = mine.shape
    units = hi - lo
    count = 4 if kind == "gelu" else 2
    out = call(
        functools.partial(across_kernel, blocks, len(arrays), lo, hi, kind),
        [mine, theirs, *arrays, *slopes],
        [jax.ShapeDtypeStruct((2 * rows, width), BF)]
        + [jax.ShapeDtypeStruct((2 * rows, units), BF)] * count,
        [pltpu.VMEM((2, width, units), BF)],
        "across_" + kind,
    )
    return out[0], list(out[1:3]), list(out[3:])


def grads_kernel(blocks, sizes, *refs):
    pairs = len(sizes)
    inputs, outs = refs[: 3 * pairs], refs[3 * pairs :]
    cut = inputs[0].shape[1] // blocks
    at = 0
    for p, size in enumerate(sizes):
        left_ref, rights = inputs[3 * p], inputs[3 * p + 1 : 3 * p + 3]
        for i in range(blocks):
            left = left_ref[:, i * cut : (i + 1) * cut]
            for half in range(2):
                value = dot(left, rights[half][...], TN)
                outs[half][i, :, at : at + size] = value.astype(BF)
        at += size


def weight_grads(place, *pairs):
    blocks = len(place.blocks)
    sizes = [rights[0].shape[1] for _, rights in pairs]
    width = pairs[0][0].shape[1]
    args = [v for left, rights in pairs for v in (left, *rights)]
    shape = jax.ShapeDtypeStruct((blocks, width // blocks, sum(sizes)), BF)
    return call(
        functools.partial(grads_kernel, blocks, sizes), args, [shape, shape], (), "grads"
    )


def back_kernel(blocks, count, lo, hi, row0, *refs):
    lefts, weights, out_ref = refs[:2], refs[2 : 2 + count], refs[2 + count]
    rows, width = out_ref.shape
    tile = min(512, rows)
    size = width // blocks

    @pl.loop(0, rows // tile)
    def _(step):
        r = pl.multiple_of(step * tile, tile)
        at = pl.ds(pl.multiple_of(row0 + step * tile, tile), tile)
        left_a, left_b = lefts[0][at, :], lefts[1][at, :]
        for i in range(blocks):
            value = dot(left_a, piece_at(weights, blocks, 0, i)[:, lo:hi], NT)
            value = value + dot(left_b, piece_at(weights, blocks, 1, i)[:, lo:hi], NT)
            out_ref[pl.ds(r, tile), i * size : (i + 1) * size] = value.astype(out_ref.dtype)


def back(lefts, gather, span, row0, rows, dtype):
    arrays = gather.arrays()
    blocks = len(gather.place.blocks)
    width = blocks * arrays[0].shape[1]
    return call(
        functools.partial(back_kernel, blocks, len(arrays), *span, row0),
        [*lefts, *arrays],
        [jax.ShapeDtypeStruct((rows, width), dtype)],
        (),
        "back",
    )[0]


def lookup_kernel(blocks, count, *refs):
    codes_refs, weights, outs = refs[:2], refs[2 : 2 + count], refs[2 + count : -1]
    w_s = refs[-1]
    rows, cols = codes_refs[0].shape[0], weights[0].shape[-1]
    size = weights[0].shape[1]
    for i in range(blocks):
        for h in range(2):
            w_s[(2 * i + h) * size : (2 * i + h + 1) * size] = piece_at(weights, blocks, h, i)[...]
    for codes_ref, out_ref in zip(codes_refs, outs):
        hot = lax.broadcasted_iota(jnp.int32, (rows, cols), 1) == codes_ref[...]
        hot = jnp.where(hot, 1.0, 0.0).astype(BF)
        out_ref[...] = dot(hot, w_s[...], NT).astype(BF)


def lookup(mine, theirs, gather):
    arrays = gather.arrays()
    blocks = len(gather.place.blocks)
    features = blocks * 2 * arrays[0].shape[1]
    shape = jax.ShapeDtypeStruct((mine.shape[0], features), BF)
    return call(
        functools.partial(lookup_kernel, blocks, len(arrays)),
        [mine, theirs, *arrays],
        [shape, shape],
        [pltpu.VMEM((features, arrays[0].shape[2]), BF)],
        "lookup",
    )


def start_kernel(blocks, factor, c_ref, mine_ref, got_ref, coded_ref, x_ref, y_ref, gains_ref):
    even = c_ref[0] == 0
    rows, width = x_ref.shape
    tile = min(64, rows)
    size = width // (2 * blocks)

    def both(at):
        mine, got = mine_ref[at, :].astype(F32), got_ref[at, :].astype(F32)
        out = []
        for i in range(blocks):
            a, b = mine[:, i * size : (i + 1) * size], got[:, i * size : (i + 1) * size]
            out += [jnp.where(even, a, b), jnp.where(even, b, a)]
        return jnp.concatenate(out, 1)

    gains_ref[...] = both(slice(rows, mine_ref.shape[0]))

    @pl.loop(0, rows // tile)
    def _(step):
        at = pl.ds(pl.multiple_of(step * tile, tile), tile)
        x = both(at) * factor + coded_ref[at, :]
        x_ref[at, :] = x
        y_ref[at, :] = (row_stats(x)[0] * gains_ref[0:1, :]).astype(BF)


def start_norm(blocks, c_index, mine, got, coded):
    rows, width = coded.shape
    vmem, smem = pl.BlockSpec(memory_space=pltpu.VMEM), pl.BlockSpec(memory_space=pltpu.SMEM)
    return pl.pallas_call(
        functools.partial(start_kernel, blocks, math.sqrt(width)),
        in_specs=[smem, vmem, vmem, vmem],
        out_specs=[vmem] * 3,
        out_shape=[
            jax.ShapeDtypeStruct((rows, width), F32),
            jax.ShapeDtypeStruct((rows, width), BF),
            jax.ShapeDtypeStruct((mine.shape[0] - rows, width), F32),
        ],
        compiler_params=pltpu.CompilerParams(vmem_limit_bytes=SMALL_VMEM),
        cost_estimate=cheap(),
        name="start",
    )(c_index, mine, got, coded)


def row_stats(x):
    centered = x - jnp.mean(x, -1, keepdims=True)
    inverse = lax.rsqrt(jnp.mean(centered * centered, -1, keepdims=True) + NORM_EPS)
    return centered * inverse, inverse


def norm_kernel(terms, *refs):
    parts, gain_ref, x_ref, y_ref = refs[:terms], refs[terms], refs[terms + 1], refs[terms + 2]
    rows = x_ref.shape[0]
    tile = min(64, rows)

    @pl.loop(0, rows // tile)
    def _(step):
        at = pl.ds(pl.multiple_of(step * tile, tile), tile)
        x = parts[0][at, :].astype(F32)
        for part in parts[1:]:
            x = x + part[at, :].astype(F32)
        x_ref[at, :] = x
        y_ref[at, :] = (row_stats(x)[0] * gain_ref[...]).astype(BF)


def norm(parts, gain):
    shape = parts[0].shape
    return call(
        functools.partial(norm_kernel, len(parts)),
        [*parts, gain],
        [jax.ShapeDtypeStruct(shape, F32), jax.ShapeDtypeStruct(shape, BF)],
        (),
        "norm",
    )


def norm_back_kernel(terms, extra, *refs):
    parts, refs = refs[:terms], refs[terms:]
    others, refs = refs[:extra], refs[extra:]
    x_ref, gain_ref, out_ref, low_ref, sum_ref = refs
    rows = x_ref.shape[0]
    tile = min(64, rows)
    sum_ref[...] = jnp.zeros_like(sum_ref)

    @pl.loop(0, rows // tile)
    def _(step):
        at = pl.ds(pl.multiple_of(step * tile, tile), tile)
        grad = parts[0][at, :].astype(F32)
        for part in parts[1:]:
            grad = grad + part[at, :].astype(F32)
        normed, inverse = row_stats(x_ref[at, :])
        scaled = grad * gain_ref[...]
        value = inverse * (
            scaled
            - jnp.mean(scaled, -1, keepdims=True)
            - normed * jnp.mean(scaled * normed, -1, keepdims=True)
        )
        for other in others:
            value = value + other[at, :]
        out_ref[at, :] = value
        low_ref[at, :] = value.astype(BF)
        sum_ref[...] += jnp.sum(grad * normed, 0, keepdims=True)


def norm_back(parts, others, x, gain):
    shape = x.shape
    return call(
        functools.partial(norm_back_kernel, len(parts), len(others)),
        [*parts, *others, x, gain],
        [
            jax.ShapeDtypeStruct(shape, F32),
            jax.ShapeDtypeStruct(shape, BF),
            jax.ShapeDtypeStruct((1, shape[1]), F32),
        ],
        (),
        "norm_back",
    )


def doc_layout(lengths_row, total_rows):
    places = jnp.arange(total_rows, dtype=jnp.int32)
    bound_one = lengths_row[0]
    bound_two = lengths_row[0] + lengths_row[1]
    doc_ids = (places >= bound_one).astype(jnp.int32) + (places >= bound_two).astype(jnp.int32)
    starts = jnp.where(doc_ids == 0, 0, jnp.where(doc_ids == 1, bound_one, bound_two))
    return (doc_ids, starts, places - starts)


def next_codes(codes_row, doc_ids, end_code):
    later = jnp.concatenate([codes_row[1:], jnp.full((1,), end_code, jnp.int32)])
    later_doc = jnp.concatenate([doc_ids[1:], jnp.full((1,), -1, jnp.int32)])
    return jnp.where(later_doc == doc_ids, later, end_code)


def head_loss(logits, targets, weights_row):
    top_score = jnp.max(logits, -1, keepdims=True)
    expo = jnp.exp(logits - top_score)
    totals = jnp.sum(expo, -1, keepdims=True)
    target_hit = jnp.arange(logits.shape[1], dtype=jnp.int32)[None, :] == targets[:, None]
    picked = jnp.sum(jnp.where(target_hit, logits, 0.0), -1)
    loss_value = jnp.sum(weights_row * (top_score[:, 0] + jnp.log(totals[:, 0]) - picked))
    grad_logits = ((expo / totals - target_hit.astype(F32)) * weights_row[:, None]).astype(BF)
    return (loss_value, grad_logits)


def adam_kernel(scale_ref, c_ref, *refs):
    correct = 1.0 - 0.5**STEP
    sources, refs = [refs[3 * i : 3 * i + 3] for i in range(6)], refs[18:]
    attn_k, attn_g, up_k, up_g, down_k, down_g, embed_ref, head_ref, gain_ref = refs[:9]
    refs = refs[9:]
    outs = [refs[4 * i : 4 + 4 * i] for i in range(6)]
    bufs = [refs[24 + 4 * i : 28 + 4 * i] for i in range(6)]
    states = [refs[48 + 3 * i : 51 + 3 * i] for i in range(6)]
    sems, in_sems = refs[66:68]
    order = (0, 2, 3, 4, 1, 5)

    def fetches(i):
        return [
            pltpu.make_async_copy(source, state, in_sems.at[i, k])
            for k, (source, state) in enumerate(zip(sources[i], states[i]))
        ]

    for i in order:
        for copy in fetches(i):
            copy.start()

    def arrive(i):
        for copy in fetches(i):
            copy.wait()

    scale = scale_ref[0]
    even = c_ref[0] == 0

    def pair(keep, got):
        return jnp.where(even, keep, got) * scale, jnp.where(even, got, keep) * scale

    def step(i, at, grad):
        master_ref, first_ref, second_ref = states[i]
        rate = RATE_GAIN if i == 5 else RATE_MATRIX
        decay = 0.0 if i == 5 else DECAY_RATE
        master = master_ref[at]
        first_new = 0.5 * first_ref[at] + 0.5 * grad
        second_new = 0.5 * second_ref[at] + 0.5 * grad * grad
        master_new = master - rate * (
            first_new / correct / (jnp.sqrt(second_new / correct) + ADAM_EPS) + decay * master
        )
        for buf, value in zip(bufs[i], (master_new, first_new, second_new, master_new.astype(BF))):
            buf[at] = value

    def copies(i):
        return [
            pltpu.make_async_copy(buf, out, sems.at[i, k])
            for k, (buf, out) in enumerate(zip(bufs[i], outs[i]))
        ]

    def send(i):
        for copy in copies(i):
            copy.start()

    every = slice(None)
    arrive(0)
    lanes = states[0][0].shape[2] // 2
    for j in range(3):
        cut = slice(j * lanes, (j + 1) * lanes)
        for k, grad in enumerate(pair(attn_k[:, cut], attn_g[:, cut])):
            step(0, (j, every, slice(k * lanes, (k + 1) * lanes)), grad)
    send(0)
    arrive(2)
    size = states[2][0].shape[1] // 2
    for k, grad in enumerate(pair(up_k[...], up_g[...])):
        step(2, (every, slice(k * size, (k + 1) * size)), grad)
    send(2)
    arrive(3)
    size = states[3][0].shape[0] // 2
    for k, grad in enumerate(pair(down_k[...], down_g[...])):
        step(3, (slice(k * size, (k + 1) * size), every), grad.T)
    send(3)
    arrive(4)
    vocab = states[4][0].shape[2]
    step(4, (0, every, every), embed_ref[:, 0:vocab] * scale)
    step(4, (1, every, every), head_ref[:, 0:vocab] * scale)
    send(4)
    arrive(1)
    size = states[1][0].shape[0] // 2
    cut = slice(3 * lanes, attn_k.shape[1])
    for k, grad in enumerate(pair(attn_k[:, cut], attn_g[:, cut])):
        step(1, (slice(k * size, (k + 1) * size), every), grad.T)
    send(1)
    arrive(5)
    step(5, (every, every), gain_ref[...] * scale)
    send(5)
    for i in range(6):
        for copy in copies(i):
            copy.wait()


def adam(scale, c_index, states, grads):
    shapes = []
    for group in states:
        shapes += [jax.ShapeDtypeStruct(group[0].shape, t) for t in (F32, F32, F32, BF)]
    args = [v for group in states for v in group] + list(grads)
    vmem, smem = pl.BlockSpec(memory_space=pltpu.VMEM), pl.BlockSpec(memory_space=pltpu.SMEM)
    hbm = pl.BlockSpec(memory_space=pl.ANY)
    return pl.pallas_call(
        adam_kernel,
        in_specs=[smem, smem] + [hbm] * 18 + [vmem] * len(grads),
        out_specs=[hbm] * len(shapes),
        out_shape=shapes,
        scratch_shapes=[pltpu.VMEM(s.shape, s.dtype) for s in shapes]
        + [pltpu.VMEM(v.shape, v.dtype) for v in args[:18]]
        + [pltpu.SemaphoreType.DMA((6, 4)), pltpu.SemaphoreType.DMA((6, 3))],
        compiler_params=pltpu.CompilerParams(vmem_limit_bytes=2 * VMEM_BYTES),
        cost_estimate=cheap(),
        name="adam",
    )(scale, c_index, *args)


def body(
    codes,
    doc_lengths,
    loss_mask,
    qkv_master,
    qkv_first,
    qkv_second,
    out_master,
    out_first,
    out_second,
    up_master,
    up_first,
    up_second,
    down_master,
    down_first,
    down_second,
    table_master,
    table_first,
    table_second,
    gain_master,
    gain_first,
    gain_second,
):
    place = Place()
    nz, ny, nb = place.nz, place.ny, len(place.blocks)
    c, z = place.c, place.z
    feat = qkv_master.shape[0]
    width = feat * place.dp
    total_rows = codes.shape[1]
    half_rows = total_rows // 2
    vocab = table_master.shape[1]
    thin = table_master.shape[2]

    joined = jnp.concatenate([codes, loss_mask, doc_lengths], 1)
    other = place.swap_c(joined)
    four = place.in_order(joined, other, 0)
    row = lax.dynamic_index_in_dim(four, z, 0, keepdims=False)
    codes_row = row[:total_rows]
    mask_row = row[total_rows : 2 * total_rows]
    lengths_row = row[2 * total_rows :]
    doc_ids, starts, local_pos = doc_layout(lengths_row, total_rows)
    targets = next_codes(codes_row, doc_ids, vocab - 1)
    first_row = c * half_rows
    my_codes = lax.dynamic_slice_in_dim(codes_row, first_row, half_rows, 0)
    my_local = lax.dynamic_slice_in_dim(local_pos, first_row, half_rows, 0)
    my_targets = lax.dynamic_slice_in_dim(targets, first_row, half_rows, 0)
    my_mask = lax.dynamic_slice_in_dim(mask_row, first_row, half_rows, 0).astype(F32)
    c_index = jnp.reshape(c, (1,)).astype(jnp.int32)
    starts_col = starts.reshape(total_rows, 1)

    def halves(matrix, axis):
        size = matrix.shape[axis] // 2
        keep = lax.dynamic_slice_in_dim(matrix, c * size, size, axis)
        send = lax.dynamic_slice_in_dim(matrix, (1 - c) * size, size, axis)
        return keep, send

    cols = -(-(vocab + 3) // 128) * 128
    table_t = jnp.swapaxes(table_master.astype(BF), 1, 2)
    embed_p = jnp.concatenate(
        [table_t[0], gain_master.astype(BF).T, jnp.zeros((thin, cols - vocab - 3), BF)], 1
    )
    head_p = jnp.concatenate([table_t[1], jnp.zeros((thin, cols - vocab), BF)], 1)
    slots = Slots()
    g_embed, g_head = Gather(place, embed_p, 0), Gather(place, head_p, 0)

    qkv_b, out_b, up_b, down_b = (
        v.astype(BF) for v in (qkv_master, out_master, up_master, down_master)
    )
    qkv_k, qkv_s = (v.reshape(feat, -1) for v in halves(qkv_b, 2))
    out_k, out_s = (v.T for v in halves(out_b, 0))
    up_k, up_s = halves(up_b, 1)
    down_k, down_s = (v.T for v in halves(down_b, 0))
    units = [v.shape[1] for v in (qkv_k, out_k, up_k, down_k)]
    keep = jnp.concatenate([qkv_k, out_k, up_k, down_k], 1)
    send = jnp.concatenate([qkv_s, out_s, up_s, down_s], 1)
    recv = place.swap_c(send)
    chip = place.in_order(keep, recv, 0)
    edges = [sum(units[:i]) for i in range(5)]
    g_attn = Gather(place, chip[:, : edges[2]], 1, [(0, units[0]), (units[0], edges[2])])
    g_up = Gather(place, chip[:, edges[2] : edges[3]], 1)
    g_down = Gather(place, chip[:, edges[3] :], 1)

    block = jnp.asarray([k for k, _ in place.blocks], jnp.int32)
    block_x = jnp.asarray([k for _, k in place.blocks], jnp.int32)
    chip_at = ((place.y + block) % ny) * 2 + (place.x ^ block_x)
    feature = (
        chip_at[:, None] * (2 * feat) + jnp.arange(2 * feat, dtype=jnp.int32)[None, :]
    ).reshape(width)
    freqs = jnp.exp((feature // 2).astype(F32) * (-2.0 * math.log(10000.0) / width))
    angles = my_local.astype(F32)[:, None] * freqs[None, :]
    coded = Cell(jnp.where((feature % 2 == 0)[None, :], jnp.sin(angles), jnp.cos(angles)))

    def branch(lefts, gather, span):
        theirs = back(lefts, gather, span, half_rows, half_rows, BF)
        got = place.swap_c(theirs)
        return back(lefts, gather, span, 0, half_rows, F32), got

    def table(gather):
        a, b = (jnp.stack(v) for v in gather.pieces())
        mine = jnp.concatenate([a, b], 1).reshape(nb, 1, nz * thin, cols)
        return place.in_order(mine, place.swap_c(mine), 1).reshape(width, cols)

    def code_rows(half):
        own = lax.dynamic_slice_in_dim(codes_row, half * half_rows, half_rows, 0)
        gain_codes = vocab + jnp.arange(16, dtype=jnp.int32)
        return jnp.concatenate([own, jnp.where(gain_codes < vocab + 3, gain_codes, -1)])[:, None]

    codes_c = cells(code_rows(c), code_rows(1 - c))
    g_attn.over_z()
    slots.slot([g_attn.near], coded, g_embed.own, *codes_c)
    g_embed.over_z()
    g_up.over_z(g_embed.parts)
    early = Slots()
    early.slot([g_embed.near])
    early.slot([g_embed.far])
    slots.slot([g_up.near, g_attn.far], *early.flight)
    g_head.over_z(g_up.parts)
    g_down.over_z(g_head.parts)
    found, found_other = lookup(codes_c[0].v, codes_c[1].v, g_embed)
    start, attn_m, gains = start_norm(nb, c_index, found, place.swap_c(found_other), coded.v)
    gains = [gains[i : i + 1] for i in range(3)]
    one_hot = (my_codes[:, None] == jnp.arange(cols, dtype=jnp.int32)[None, :]).astype(BF)
    attn_c, other_c = cells(attn_m, place.swap_c(attn_m))

    slots.slot([g_down.near, g_up.far], attn_c, other_c)
    span_qkv = (0, nz // 2 * units[0])
    span_out = (span_qkv[1], nz // 2 * edges[2])
    span_up, span_down = (0, nz // 2 * units[2]), (0, nz // 2 * units[3])
    attn_in, qkv, _ = across(attn_c.v, other_c.v, g_attn, span_qkv)
    mixed, lse = zip(*(attention(c_index, starts_col, v) for v in qkv))
    theirs_c = Cell(back(mixed, g_attn, span_out, half_rows, half_rows, BF))
    mine_c = Cell(back(mixed, g_attn, span_out, 0, half_rows, F32))

    slots.slot([g_head.near, g_down.far], theirs_c, mine_c)
    middle, ffn_m = norm([start, mine_c.v, place.swap_c(theirs_c.v)], gains[1])
    ffn_in, hidden, slope = across(ffn_m, place.swap_c(ffn_m), g_up, span_up, "gelu")
    hidden_c = cells(*hidden)
    slots.slot([g_head.far], *hidden_c)
    hidden = [v.v for v in hidden_c]
    final, features = norm([middle, *branch(hidden, g_down, span_down)], gains[2])
    a, b = (jnp.stack(v) for v in g_head.pieces())
    mine = jnp.concatenate([a, b], 1).reshape(nb, 1, nz * thin, cols)
    head_t = place.in_order(mine, place.swap_c(mine), 1).reshape(width, cols)
    logits = dot(features, head_t)
    logits = jnp.where(jnp.arange(cols)[None, :] < vocab, logits, -1e30)
    loss_local, grad_logits = head_loss(logits, my_targets, my_mask)

    slots = Slots()
    cut = 2 * feat

    def matrix_sum(*pairs):
        whole = weight_grads(place, *pairs)
        groups, start_at = [], 0
        for _, rights in pairs:
            size = rights[0].shape[1] // (nz // 2)
            groups.append((start_at, start_at + size))
            start_at += size
        return Reduce(place, whole, 1, groups)

    def table_sum(left, right, extra=None):
        def by_c(values):
            size = nz * thin
            even, odd = (
                jnp.concatenate([values[..., (2 * i + k) * size : (2 * i + k + 1) * size] for i in range(nb)], -1)
                for k in (0, 1)
            )
            return jnp.where(c == 0, even, odd), jnp.where(c == 0, odd, even)

        left_k, left_s = by_c(left)
        own = dot(left_k, right, TN)
        sent = dot(left_s, right, TN)
        if extra is not None:
            extra_k, extra_s = (
                jnp.pad(v.T, ((0, 0), (vocab, cols - vocab - extra.shape[0]))) for v in by_c(extra)
            )
            own, sent = own + extra_k, sent + extra_s
        got = place.swap_c(sent.astype(BF))
        chip_sum = (own + got.astype(F32)).astype(BF).reshape(nb, 2, nz // 2 * thin, cols)
        return Reduce(place, [chip_sum[:, 0], chip_sum[:, 1]], 0)

    r_head = table_sum(features, grad_logits)
    grad_feat = dot(grad_logits, head_t, NT)
    grad_final, grad_down, gain_three = norm_back([grad_feat], [], final, gains[2])
    grad_down_c, other_c = cells(grad_down, place.swap_c(grad_down))
    slots.slot([r_head.near], grad_down_c, other_c)
    grad_down, other = grad_down_c.v, other_c.v
    r_down = matrix_sum((jnp.concatenate([grad_down, other], 0), hidden))

    grad_down_c, other_c = cells(grad_down, other)
    slots.slot([r_down.near, r_head.far], grad_down_c, other_c)
    _, grad_up, _ = across(grad_down_c.v, other_c.v, g_down, span_down, "slope", slope)
    theirs_c = Cell(back(grad_up, g_up, span_up, half_rows, half_rows, BF))
    mine_c = Cell(back(grad_up, g_up, span_up, 0, half_rows, F32))
    r_up = matrix_sum((ffn_in, grad_up))

    slots.slot([r_up.near, r_down.far], theirs_c, mine_c)
    grad_mid, grad_out, gain_two = norm_back(
        [mine_c.v, place.swap_c(theirs_c.v)], [grad_final], middle, gains[1]
    )
    grad_out, grad_mixed, _ = across(grad_out, place.swap_c(grad_out), g_attn, span_out)
    grad_qkv = [
        attention_back(c_index, starts_col, q, o, g, ls)
        for q, o, g, ls in zip(qkv, mixed, grad_mixed, lse)
    ]
    r_attn = matrix_sum((attn_in, grad_qkv), (grad_out, mixed))
    theirs_c = Cell(back(grad_qkv, g_attn, span_qkv, half_rows, half_rows, BF))
    mine_c = Cell(back(grad_qkv, g_attn, span_qkv, 0, half_rows, F32))

    slots.slot([r_attn.near, r_up.far], theirs_c, mine_c)
    r_down.over_z()
    grad_start, _, gain_one = norm_back(
        [mine_c.v, place.swap_c(theirs_c.v)], [grad_mid], start, gains[0]
    )
    gain_grad = jnp.concatenate([gain_one, gain_two, gain_three], 0)
    r_embed = table_sum((grad_start * math.sqrt(width)).astype(BF), one_hot, gain_grad)

    slots.slot([r_attn.far, r_embed.near])
    r_up.over_z(r_down.got)
    slots.slot([r_embed.far])
    r_head.over_z(slots.flight[0])
    r_attn.over_z(r_up.got)
    r_embed.over_z(r_up.got)

    def shards(total):
        keep_g, send_g = halves(total, 0)
        return keep_g, place.swap_c(send_g)

    head_sum, down_sum, up_sum = r_head.result(), r_down.result(), r_up.result()
    down_k, down_g = shards(down_sum)
    up_k, up_g = shards(up_sum)
    attn_sum = r_attn.result()
    attn_k, attn_g = shards(attn_sum)
    embed_sum = r_embed.result()
    squares = sum(
        jnp.sum(v * v) for v in (head_sum, down_sum, up_sum, attn_sum, embed_sum)
    )
    stats = jnp.stack([loss_local, jnp.sum(my_mask), squares])
    stats = place.total(stats)
    loss_all, count_all = stats[0], stats[1]
    norm_all = jnp.sqrt(stats[2] / (count_all * count_all))
    factor = jnp.minimum(1.0, CLIP_NORM / (norm_all + 1e-06))
    scale = jnp.reshape(factor / count_all, (1,))
    states = (
        [jnp.swapaxes(v, 0, 1) for v in (qkv_master, qkv_first, qkv_second)],
        (out_master, out_first, out_second),
        (up_master, up_first, up_second),
        (down_master, down_first, down_second),
        [jnp.swapaxes(v, 1, 2) for v in (table_master, table_first, table_second)],
        (gain_master, gain_first, gain_second),
    )
    gain_sum = embed_sum[:, vocab : vocab + 3].T
    grads = (attn_k, attn_g, up_k, up_g, down_k, down_g, embed_sum, head_sum, gain_sum)
    new = list(adam(scale, c_index, states, grads))
    new[0:4] = [jnp.swapaxes(v, 0, 1) for v in new[0:4]]
    new[16:20] = [jnp.swapaxes(v, 1, 2) for v in new[16:20]]
    return tuple(new) + (loss_all, count_all, norm_all)


def solution(mesh):
    rows, cols = P("dp", None, "tensor"), P("tensor", "dp")
    plain, both, gain = P("dp", "tensor"), P(None, None, ("dp", "tensor")), P(None, ("dp", "tensor"))
    kinds = (rows, cols, plain, cols, both, gain)
    in_specs = (P("dp", None),) * 3 + tuple(k for k in kinds for _ in range(3))
    out_specs = tuple(k for k in kinds for _ in range(4)) + (P(),) * 3
    return jax.shard_map(body, mesh=mesh, in_specs=in_specs, out_specs=out_specs, check_vma=False)
```

```python
import functools
import math

import jax
import jax.numpy as jnp
from jax import lax
from jax.experimental import pallas as pl
from jax.experimental.pallas import tpu as pltpu
from jax.sharding import PartitionSpec as P

HEAD = 64
STEP = 5

RATE_MATRIX = 0.03
RATE_GAIN = 0.25
DECAY_RATE = 0.01
CLIP_NORM = 0.002
NORM_EPS = 1e-05
ADAM_EPS = 1e-08

BF = jnp.bfloat16
F32 = jnp.float32
LOG2E = math.log2(math.e)
NN = (((1,), (0,)), ((), ()))
NT = (((1,), (1,)), ((), ()))
TN = (((0,), (0,)), ((), ()))
VMEM_BYTES = 28 * 1024 * 1024
SMALL_VMEM = 24 * 1024 * 1024


def dot(left, right, dims=NN):
    return lax.dot_general(left, right, dims, preferred_element_type=F32)


def barrier(*values):
    return lax.optimization_barrier(values)


class Place:
    def __init__(self):
        self.dp = lax.axis_size("dp")
        self.nz = lax.axis_size("tensor")
        self.ny = self.dp // 4
        index = lax.axis_index("dp")
        self.z = lax.axis_index("tensor")
        self.c = index % 2
        self.x = (index // 2) % 2
        self.y = index // 4
        self.blocks = [(0, 0), (0, 1)]
        self.blocks += [(k, 1) for k in range(1, self.ny)]
        self.blocks += [(k, 0) for k in range(1, self.ny)]

    def at(self, ky, kx):
        return self.blocks.index((ky, kx))

    def swap_c(self, value):
        return lax.ppermute(value, "dp", [(i, i ^ 1) for i in range(self.dp)])

    def swap_x(self, value):
        return lax.ppermute(value, "dp", [(i, i ^ 2) for i in range(self.dp)])

    def from_y(self, value, k):
        n = self.dp
        return lax.ppermute(value, "dp", [((i + 4 * k) % n, i) for i in range(n)])

    def to_y(self, value, k):
        n = self.dp
        return lax.ppermute(value, "dp", [(i, (i + 4 * k) % n) for i in range(n)])

    def from_z(self, value, k):
        n = self.nz
        return lax.ppermute(value, "tensor", [((i + k) % n, i) for i in range(n)])

    def to_z(self, value, k):
        n = self.nz
        return lax.ppermute(value, "tensor", [(i, (i + k) % n) for i in range(n)])

    def all_z(self, value):
        return lax.all_to_all(value, "tensor", 0, 0)

    def from_block(self, value, block):
        (ky, kx), n = block, self.dp
        return lax.ppermute(value, "dp", [(((i ^ (2 * kx)) + 4 * ky) % n, i) for i in range(n)])

    def total(self, value):
        value = value + self.swap_c(value)
        n = self.dp
        around = [
            lax.ppermute(value, "dp", [(((i ^ (2 * kx)) + 4 * ky) % n, i) for i in range(n)])
            for ky, kx in self.blocks[1:]
        ]
        value = value + sum(around)
        return value + sum(self.from_z(value, k) for k in range(1, self.nz))

    def in_order(self, mine, other, axis):
        first = jnp.where(self.c == 0, mine, other)
        last = jnp.where(self.c == 0, other, mine)
        return jnp.concatenate([first, last], axis)


class Cell:
    def __init__(self, value):
        self.v = value


def cells(*values):
    return [Cell(v) for v in values]


def fence(*held):
    held = list(dict.fromkeys(held))
    for cell, value in zip(held, barrier(*[c.v for c in held])):
        cell.v = value


class Slots:
    def __init__(self):
        self.flight = []

    def slot(self, stages, *also, wait=True):
        plans = [stage() for stage in stages]
        sends = [s for plan, _ in plans for s in plan]
        fence(*(self.flight if wait else ()), *[c for _, c in sends], *also)
        out = [Cell(send(c.v)) for send, c in sends]
        self.flight = out if wait else self.flight + out
        at = 0
        for plan, take in plans:
            take(out[at : at + len(plan)])
            at += len(plan)


class Gather:
    def __init__(self, place, own, axis, groups=None):
        self.place, self.own, self.axis, self.groups = place, Cell(own), axis, groups
        self.wide = Cell(jnp.broadcast_to(own[None], (place.nz,) + own.shape))
        self.ks = range(1, place.ny)

    def over_z(self, *after):
        fence(self.wide, *after)
        self.parts = Cell(self.place.all_z(self.wide.v))

    def near(self):
        place, half = self.place, self.place.nz // 2
        parts, groups = self.parts.v, self.groups or [(0, self.own.v.shape[1])]
        self.both = Cell(
            jnp.stack(
                [
                    jnp.concatenate(
                        [parts[i][:, g0:g1] for g0, g1 in groups for i in range(lo, lo + half)],
                        self.axis,
                    )
                    for lo in (0, half)
                ]
            )
        )

        def take(out):
            self.by_x, self.by_y = out[0], out[1:]

        plan = [(place.swap_x, self.both)]
        return plan + [(functools.partial(place.from_y, k=k), self.both) for k in self.ks], take

    def far(self):
        place = self.place

        def take(out):
            self.far_a, self.far_b = out[: place.ny - 1], out[place.ny - 1 :]

        plan = [(lambda v: place.swap_x(v[0]), v) for v in self.by_y]
        return plan + [(lambda v, k=k: place.from_y(v[1], k), self.by_x) for k in self.ks], take

    def pieces(self):
        out = []
        for half, far in ((0, self.far_a), (1, self.far_b)):
            out.append(
                [self.both.v[half], self.by_x.v[half]]
                + [v.v for v in far]
                + [v.v[half] for v in self.by_y]
            )
        return out

    def arrays(self):
        cells = [self.both, self.by_x, *self.far_a, *self.far_b, *self.by_y]
        return [c.v for c in cells]


class Reduce:
    def __init__(self, place, whole, axis, groups=None):
        self.place, self.whole, self.axis, self.groups = place, whole, axis, groups
        self.ks = range(1, place.ny)

    def near(self):
        place = self.place
        a, b = self.whole

        def take(out):
            self.got_a, self.got_b = out[0], out[1:]

        plan = [(place.swap_x, Cell(a[1 : 1 + place.ny]))]
        for k in self.ks:
            if place.ny == 2:
                sent = b[2:4]
            else:
                sent = jnp.stack([b[place.at(k, 1)], b[place.at(k, 0)]])
            plan.append((functools.partial(place.to_y, k=k), Cell(sent)))
        return plan, take

    def far(self):
        place = self.place
        a, b = self.whole

        def take(out):
            self.far_a, self.far_b = out[:-1], out[-1]

        def along(got, k):
            sent = a[place.at(k, 0)].astype(F32) + got[k].astype(F32)
            return place.to_y(sent.astype(BF), k)

        def across(first):
            sent = b[1].astype(F32) + first[0].astype(F32)
            for other in self.got_b[1:]:
                sent = sent + other.v[0].astype(F32)
            return place.swap_x(sent.astype(BF))

        plan = [(functools.partial(along, k=k), self.got_a) for k in self.ks]
        return plan + [(across, self.got_b[0])], take

    def over_z(self, *after):
        place, half = self.place, self.place.nz // 2
        a, b = self.whole
        own_a = a[0].astype(F32) + self.got_a.v[0].astype(F32) + sum(v.v.astype(F32) for v in self.far_a)
        own_b = (
            b[0].astype(F32) + sum(v.v[1].astype(F32) for v in self.got_b) + self.far_b.v.astype(F32)
        )
        if self.axis == 0:
            chunks = jnp.split(own_a, half, 0) + jnp.split(own_b, half, 0)
        else:
            chunks = []
            for own in (own_a, own_b):
                parts = [jnp.split(own[:, half * g0 : half * g1], half, 1) for g0, g1 in self.groups]
                chunks += [jnp.concatenate(v, 1) for v in zip(*parts)]
        sent = Cell(jnp.stack([v.astype(BF) for v in chunks]))
        fence(sent, *after)
        if self.axis == 0:
            pieces = [
                lax.dynamic_index_in_dim(sent.v, (place.z + k) % place.nz, 0, keepdims=False)
                for k in range(place.nz)
            ]
            moved = [place.to_z(pieces[k], k) for k in range(1, place.nz)]
            self.got = Cell(jnp.stack(pieces[:1] + moved))
        else:
            self.got = Cell(place.all_z(sent.v))

    def result(self):
        return jnp.sum(self.got.v.astype(F32), 0)


class GatherTable:
    def __init__(self, place, own):
        self.place, self.own = place, own

    def over_z(self):
        place, own = self.place, self.own
        parts = [own] + [place.from_z(own, k) for k in range(1, place.nz)]
        parts = jnp.roll(jnp.stack(parts), place.z, 0)
        self.parts = Cell(parts.reshape(-1, own.shape[1]))

    def around(self):
        place = self.place

        def take(out):
            self.others = out

        return [
            (functools.partial(place.from_block, block=block), self.parts) for block in place.blocks[1:]
        ], take

    def arrays(self):
        return [c.v for c in [self.parts] + self.others]


def forward_kernel(c_ref, start_ref, qkv_ref, o_ref, lse_ref, k_s, v_s):
    c = c_ref[0]
    half = qkv_ref.shape[1]
    total = 2 * half
    block = min(256, half)
    per_half = half // block
    scale = HEAD ** (-0.5) * LOG2E
    for b in range(2):
        k_s[b * half : (b + 1) * half] = qkv_ref[b ^ c, :, 128:256]
        v_s[b * half : (b + 1) * half] = qkv_ref[b ^ c, :, 256:384]
    lane = lax.broadcasted_iota(jnp.int32, (block, 128), 1)
    for qb in range(total // block):
        rel = (qb // per_half) ^ c
        r0 = (qb % per_half) * block
        n = (qb + 1) * block
        q = qkv_ref[rel, r0 : r0 + block, 0:128]
        row = qb * block + lax.broadcasted_iota(jnp.int32, (block, n), 0)
        col = lax.broadcasted_iota(jnp.int32, (block, n), 1)
        start = start_ref[qb * block : (qb + 1) * block, 0:1]
        allowed = (col >= start) & (col <= row)
        outs = []
        for h in range(2):
            qh = jnp.where((lane >= 64) == (h == 1), q, jnp.zeros_like(q))
            s = dot(qh, k_s[0:n], NT)
            s = jnp.where(allowed, s, -1e30)
            top = jnp.max(s, -1, keepdims=True)
            p = jnp.exp2((s - top) * scale)
            total_p = jnp.sum(p, -1, keepdims=True)
            outs.append(dot(p.astype(BF), v_s[0:n]) / total_p)
            lse = top * scale + jnp.log2(total_p)
            lse_ref[0, qb * block : (qb + 1) * block, h * 64 : (h + 1) * 64] = jnp.broadcast_to(
                lse, (block, 64)
            )
        o_ref[rel, r0 : r0 + block, :] = jnp.where(lane < 64, outs[0], outs[1]).astype(BF)


def backward_kernel(c_ref, start_ref, qkv_ref, o_ref, go_ref, lse_ref, out_ref, k_s, v_s, gk_s, gv_s):
    c = c_ref[0]
    half = qkv_ref.shape[1]
    total = 2 * half
    block = min(256, half)
    per_half = half // block
    scale = HEAD ** (-0.5)
    for b in range(2):
        k_s[b * half : (b + 1) * half] = qkv_ref[b ^ c, :, 128:256]
        v_s[b * half : (b + 1) * half] = qkv_ref[b ^ c, :, 256:384]
    lane = lax.broadcasted_iota(jnp.int32, (block, 128), 1)
    for step, qb in enumerate(reversed(range(total // block))):
        rel = (qb // per_half) ^ c
        r0 = (qb % per_half) * block
        n = (qb + 1) * block
        q = qkv_ref[rel, r0 : r0 + block, 0:128]
        go = go_ref[rel, r0 : r0 + block, :]
        o = o_ref[rel, r0 : r0 + block, :]
        row = qb * block + lax.broadcasted_iota(jnp.int32, (block, n), 0)
        col = lax.broadcasted_iota(jnp.int32, (block, n), 1)
        start = start_ref[qb * block : (qb + 1) * block, 0:1]
        allowed = (col >= start) & (col <= row)
        both = go.astype(F32) * o.astype(F32)
        gq = None
        for h in range(2):
            mine = (lane >= 64) == (h == 1)
            qh = jnp.where(mine, q, jnp.zeros_like(q))
            gh = jnp.where(mine, go, jnp.zeros_like(go))
            s = dot(qh, k_s[0:n], NT)
            lse = lse_ref[0, qb * block : (qb + 1) * block, h * 64 : h * 64 + 1]
            p = jnp.where(allowed, jnp.exp2(jnp.minimum(s * (scale * LOG2E) - lse, 1.0)), 0.0)
            gp = dot(gh, v_s[0:n], NT)
            inner = jnp.sum(jnp.where(mine, both, 0.0), -1, keepdims=True)
            gs = (p * (gp - inner)).astype(BF)
            pb = p.astype(BF)
            gqh = dot(gs, k_s[0:n])
            gq = gqh if gq is None else jnp.where(lane < 64, gq, gqh)
            gk = dot(gs, qh, TN)
            gv = dot(pb, gh, TN)
            if step == 0 and h == 0:
                gk_s[0:n] = gk
                gv_s[0:n] = gv
            else:
                gk_s[0:n] += gk
                gv_s[0:n] += gv
        out_ref[rel, r0 : r0 + block, 0:128] = (gq * scale).astype(BF)
    for b in range(2):
        out_ref[b ^ c, :, 128:256] = (gk_s[b * half : (b + 1) * half] * scale).astype(BF)
        out_ref[b ^ c, :, 256:384] = gv_s[b * half : (b + 1) * half].astype(BF)


def attention(c_index, starts, qkv):
    rows, cols = qkv.shape
    half, pairs = rows // 2, cols // 384
    smem = pl.BlockSpec(memory_space=pltpu.SMEM)
    out, lse = pl.pallas_call(
        forward_kernel,
        grid=(pairs,),
        in_specs=[
            smem,
            pl.BlockSpec((rows, 1), lambda j: (0, 0)),
            pl.BlockSpec((2, half, 384), lambda j: (0, 0, j)),
        ],
        out_specs=[
            pl.BlockSpec((2, half, 128), lambda j: (0, 0, j)),
            pl.BlockSpec((1, rows, 128), lambda j: (j, 0, 0)),
        ],
        out_shape=[
            jax.ShapeDtypeStruct((2, half, pairs * 128), BF),
            jax.ShapeDtypeStruct((pairs, rows, 128), F32),
        ],
        scratch_shapes=[pltpu.VMEM((rows, 128), BF), pltpu.VMEM((rows, 128), BF)],
        compiler_params=pltpu.CompilerParams(vmem_limit_bytes=VMEM_BYTES),
        cost_estimate=pl.CostEstimate(
            flops=1, bytes_accessed=1, transcendentals=0
        ),
        name="attend",
    )(c_index, starts, qkv.reshape(2, half, cols))
    return out.reshape(rows, pairs * 128), lse


def attention_back(c_index, starts, qkv, out, grad, lse):
    rows, cols = qkv.shape
    half, pairs = rows // 2, cols // 384
    smem = pl.BlockSpec(memory_space=pltpu.SMEM)
    wide = pl.BlockSpec((2, half, 384), lambda j: (0, 0, j))
    thin = pl.BlockSpec((2, half, 128), lambda j: (0, 0, j))
    result = pl.pallas_call(
        backward_kernel,
        grid=(pairs,),
        in_specs=[
            smem,
            pl.BlockSpec((rows, 1), lambda j: (0, 0)),
            wide,
            thin,
            thin,
            pl.BlockSpec((1, rows, 128), lambda j: (j, 0, 0)),
        ],
        out_specs=wide,
        out_shape=jax.ShapeDtypeStruct((2, half, cols), BF),
        scratch_shapes=[
            pltpu.VMEM((rows, 128), BF),
            pltpu.VMEM((rows, 128), BF),
            pltpu.VMEM((rows, 128), F32),
            pltpu.VMEM((rows, 128), F32),
        ],
        compiler_params=pltpu.CompilerParams(vmem_limit_bytes=VMEM_BYTES),
        cost_estimate=pl.CostEstimate(
            flops=1, bytes_accessed=1, transcendentals=0
        ),
        name="attend_back",
    )(
        c_index,
        starts,
        qkv.reshape(2, half, cols),
        out.reshape(2, half, pairs * 128),
        grad.reshape(2, half, pairs * 128),
        lse,
    )
    return result.reshape(rows, cols)


def cheap():
    return pl.CostEstimate(flops=1, bytes_accessed=1, transcendentals=0)


def call(kernel, args, shapes, scratch=(), name=None):
    vmem = pl.BlockSpec(memory_space=pltpu.VMEM)
    return pl.pallas_call(
        kernel,
        in_specs=[vmem] * len(args),
        out_specs=[vmem] * len(shapes),
        out_shape=shapes,
        scratch_shapes=list(scratch),
        compiler_params=pltpu.CompilerParams(vmem_limit_bytes=SMALL_VMEM),
        cost_estimate=cheap(),
        name=name,
    )(*args)


def piece_at(refs, blocks, half, i):
    far = (blocks - 2) // 2
    if i < 2:
        return refs[i].at[half]
    if i < 2 + far:
        return refs[i + half * far]
    return refs[i + far].at[half]


def gelu_parts(value):
    phi = 0.5 * (1.0 + lax.erf(value * (0.5**0.5)))
    slope = phi + value * (jnp.exp(-0.5 * value * value) * (1.0 / math.sqrt(2.0 * math.pi)))
    return value * phi, slope


def across_kernel(blocks, count, lo, hi, kind, *refs):
    mine_ref, theirs_ref = refs[:2]
    weights = refs[2 : 2 + count]
    refs = refs[2 + count :]
    slopes = ()
    if kind == "slope":
        slopes, refs = refs[:2], refs[2:]
    joined_ref, refs = refs[0], refs[1:]
    outs, w_s = refs[:-1], refs[-1]
    rows = mine_ref.shape[0]
    tile = min(512, rows)
    size = w_s.shape[1] // blocks
    for half in range(2):
        for i in range(blocks):
            w_s[half, i * size : (i + 1) * size] = piece_at(weights, blocks, half, i)[:, lo:hi]
    for base, source in ((0, mine_ref), (rows, theirs_ref)):

        @pl.loop(0, rows // tile)
        def _(step):
            r = pl.multiple_of(step * tile, tile)
            at = pl.ds(pl.multiple_of(base + step * tile, tile), tile)
            left = source[pl.ds(r, tile), :]
            joined_ref[at, :] = left
            for half in range(2):
                value = dot(left, w_s[half])
                if kind == "gelu":
                    value, slope = gelu_parts(value)
                    outs[2 + half][at, :] = slope.astype(BF)
                elif kind == "slope":
                    value = value * slopes[half][at, :].astype(F32)
                outs[half][at, :] = value.astype(BF)


def across(mine, theirs, gather, span, kind="plain", slopes=()):
    arrays = gather.arrays()
    blocks = len(gather.place.blocks)
    lo, hi = span
    rows, width = mine.shape
    units = hi - lo
    count = 4 if kind == "gelu" else 2
    out = call(
        functools.partial(across_kernel, blocks, len(arrays), lo, hi, kind),
        [mine, theirs, *arrays, *slopes],
        [jax.ShapeDtypeStruct((2 * rows, width), BF)]
        + [jax.ShapeDtypeStruct((2 * rows, units), BF)] * count,
        [pltpu.VMEM((2, width, units), BF)],
        "across_" + kind,
    )
    return out[0], list(out[1:3]), list(out[3:])


def grads_kernel(blocks, sizes, *refs):
    pairs = len(sizes)
    inputs, outs = refs[: 3 * pairs], refs[3 * pairs :]
    cut = inputs[0].shape[1] // blocks
    at = 0
    for p, size in enumerate(sizes):
        left_ref, rights = inputs[3 * p], inputs[3 * p + 1 : 3 * p + 3]
        for i in range(blocks):
            left = left_ref[:, i * cut : (i + 1) * cut]
            for half in range(2):
                value = dot(left, rights[half][...], TN)
                outs[half][i, :, at : at + size] = value.astype(BF)
        at += size


def weight_grads(place, *pairs):
    blocks = len(place.blocks)
    sizes = [rights[0].shape[1] for _, rights in pairs]
    width = pairs[0][0].shape[1]
    args = [v for left, rights in pairs for v in (left, *rights)]
    shape = jax.ShapeDtypeStruct((blocks, width // blocks, sum(sizes)), BF)
    return call(
        functools.partial(grads_kernel, blocks, sizes), args, [shape, shape], (), "grads"
    )


def back_kernel(blocks, count, lo, hi, row0, *refs):
    lefts, weights, out_ref = refs[:2], refs[2 : 2 + count], refs[2 + count]
    rows, width = out_ref.shape
    tile = min(512, rows)
    size = width // blocks

    @pl.loop(0, rows // tile)
    def _(step):
        r = pl.multiple_of(step * tile, tile)
        at = pl.ds(pl.multiple_of(row0 + step * tile, tile), tile)
        left_a, left_b = lefts[0][at, :], lefts[1][at, :]
        for i in range(blocks):
            value = dot(left_a, piece_at(weights, blocks, 0, i)[:, lo:hi], NT)
            value = value + dot(left_b, piece_at(weights, blocks, 1, i)[:, lo:hi], NT)
            out_ref[pl.ds(r, tile), i * size : (i + 1) * size] = value.astype(out_ref.dtype)


def back(lefts, gather, span, row0, rows, dtype):
    arrays = gather.arrays()
    blocks = len(gather.place.blocks)
    width = blocks * arrays[0].shape[1]
    return call(
        functools.partial(back_kernel, blocks, len(arrays), *span, row0),
        [*lefts, *arrays],
        [jax.ShapeDtypeStruct((rows, width), dtype)],
        (),
        "back",
    )[0]


def lookup_kernel(blocks, count, *refs):
    codes_refs, weights, outs = refs[:2], refs[2 : 2 + count], refs[2 + count : -1]
    w_s = refs[-1]
    rows, cols = codes_refs[0].shape[0], weights[0].shape[-1]
    size = weights[0].shape[0]
    for i in range(blocks):
        w_s[i * size : (i + 1) * size] = weights[i][...]
    for codes_ref, out_ref in zip(codes_refs, outs):
        hot = lax.broadcasted_iota(jnp.int32, (rows, cols), 1) == codes_ref[...]
        hot = jnp.where(hot, 1.0, 0.0).astype(BF)
        out_ref[...] = dot(hot, w_s[...], NT).astype(BF)


def lookup(mine, theirs, gather):
    arrays = gather.arrays()
    blocks = len(gather.place.blocks)
    features = blocks * arrays[0].shape[0]
    shape = jax.ShapeDtypeStruct((mine.shape[0], features), BF)
    return call(
        functools.partial(lookup_kernel, blocks, len(arrays)),
        [mine, theirs, *arrays],
        [shape, shape],
        [pltpu.VMEM((features, arrays[0].shape[1]), BF)],
        "lookup",
    )


def start_kernel(blocks, factor, c_ref, mine_ref, got_ref, coded_ref, x_ref, y_ref, gains_ref):
    even = c_ref[0] == 0
    rows, width = x_ref.shape
    tile = min(64, rows)
    size = width // (2 * blocks)

    def both(at):
        mine, got = mine_ref[at, :].astype(F32), got_ref[at, :].astype(F32)
        out = []
        for i in range(blocks):
            a, b = mine[:, i * size : (i + 1) * size], got[:, i * size : (i + 1) * size]
            out += [jnp.where(even, a, b), jnp.where(even, b, a)]
        return jnp.concatenate(out, 1)

    gains_ref[...] = both(slice(rows, mine_ref.shape[0]))

    @pl.loop(0, rows // tile)
    def _(step):
        at = pl.ds(pl.multiple_of(step * tile, tile), tile)
        x = both(at) * factor + coded_ref[at, :]
        x_ref[at, :] = x
        y_ref[at, :] = (row_stats(x)[0] * gains_ref[0:1, :]).astype(BF)


def start_norm(blocks, c_index, mine, got, coded):
    rows, width = coded.shape
    vmem, smem = pl.BlockSpec(memory_space=pltpu.VMEM), pl.BlockSpec(memory_space=pltpu.SMEM)
    return pl.pallas_call(
        functools.partial(start_kernel, blocks, math.sqrt(width)),
        in_specs=[smem, vmem, vmem, vmem],
        out_specs=[vmem] * 3,
        out_shape=[
            jax.ShapeDtypeStruct((rows, width), F32),
            jax.ShapeDtypeStruct((rows, width), BF),
            jax.ShapeDtypeStruct((mine.shape[0] - rows, width), F32),
        ],
        compiler_params=pltpu.CompilerParams(vmem_limit_bytes=SMALL_VMEM),
        cost_estimate=cheap(),
        name="start",
    )(c_index, mine, got, coded)


def row_stats(x):
    centered = x - jnp.mean(x, -1, keepdims=True)
    inverse = lax.rsqrt(jnp.mean(centered * centered, -1, keepdims=True) + NORM_EPS)
    return centered * inverse, inverse


def norm_kernel(terms, *refs):
    parts, gain_ref, x_ref, y_ref = refs[:terms], refs[terms], refs[terms + 1], refs[terms + 2]
    rows = x_ref.shape[0]
    tile = min(64, rows)

    @pl.loop(0, rows // tile)
    def _(step):
        at = pl.ds(pl.multiple_of(step * tile, tile), tile)
        x = parts[0][at, :].astype(F32)
        for part in parts[1:]:
            x = x + part[at, :].astype(F32)
        x_ref[at, :] = x
        y_ref[at, :] = (row_stats(x)[0] * gain_ref[...]).astype(BF)


def norm(parts, gain):
    shape = parts[0].shape
    return call(
        functools.partial(norm_kernel, len(parts)),
        [*parts, gain],
        [jax.ShapeDtypeStruct(shape, F32), jax.ShapeDtypeStruct(shape, BF)],
        (),
        "norm",
    )


def norm_back_kernel(terms, extra, *refs):
    parts, refs = refs[:terms], refs[terms:]
    others, refs = refs[:extra], refs[extra:]
    x_ref, gain_ref, out_ref, low_ref, sum_ref = refs
    rows = x_ref.shape[0]
    tile = min(64, rows)
    sum_ref[...] = jnp.zeros_like(sum_ref)

    @pl.loop(0, rows // tile)
    def _(step):
        at = pl.ds(pl.multiple_of(step * tile, tile), tile)
        grad = parts[0][at, :].astype(F32)
        for part in parts[1:]:
            grad = grad + part[at, :].astype(F32)
        normed, inverse = row_stats(x_ref[at, :])
        scaled = grad * gain_ref[...]
        value = inverse * (
            scaled
            - jnp.mean(scaled, -1, keepdims=True)
            - normed * jnp.mean(scaled * normed, -1, keepdims=True)
        )
        for other in others:
            value = value + other[at, :]
        out_ref[at, :] = value
        low_ref[at, :] = value.astype(BF)
        sum_ref[...] += jnp.sum(grad * normed, 0, keepdims=True)


def norm_back(parts, others, x, gain):
    shape = x.shape
    return call(
        functools.partial(norm_back_kernel, len(parts), len(others)),
        [*parts, *others, x, gain],
        [
            jax.ShapeDtypeStruct(shape, F32),
            jax.ShapeDtypeStruct(shape, BF),
            jax.ShapeDtypeStruct((1, shape[1]), F32),
        ],
        (),
        "norm_back",
    )


def doc_layout(lengths_row, total_rows):
    places = jnp.arange(total_rows, dtype=jnp.int32)
    bound_one = lengths_row[0]
    bound_two = lengths_row[0] + lengths_row[1]
    doc_ids = (places >= bound_one).astype(jnp.int32) + (places >= bound_two).astype(jnp.int32)
    starts = jnp.where(doc_ids == 0, 0, jnp.where(doc_ids == 1, bound_one, bound_two))
    return (doc_ids, starts, places - starts)


def next_codes(codes_row, doc_ids, end_code):
    later = jnp.concatenate([codes_row[1:], jnp.full((1,), end_code, jnp.int32)])
    later_doc = jnp.concatenate([doc_ids[1:], jnp.full((1,), -1, jnp.int32)])
    return jnp.where(later_doc == doc_ids, later, end_code)


def head_loss(logits, targets, weights_row):
    top_score = jnp.max(logits, -1, keepdims=True)
    expo = jnp.exp(logits - top_score)
    totals = jnp.sum(expo, -1, keepdims=True)
    target_hit = jnp.arange(logits.shape[1], dtype=jnp.int32)[None, :] == targets[:, None]
    picked = jnp.sum(jnp.where(target_hit, logits, 0.0), -1)
    loss_value = jnp.sum(weights_row * (top_score[:, 0] + jnp.log(totals[:, 0]) - picked))
    grad_logits = ((expo / totals - target_hit.astype(F32)) * weights_row[:, None]).astype(BF)
    return (loss_value, grad_logits)


def adam_kernel(scale_ref, c_ref, *refs):
    correct = 1.0 - 0.5**STEP
    sources, refs = [refs[3 * i : 3 * i + 3] for i in range(6)], refs[18:]
    attn_k, attn_g, up_k, up_g, down_k, down_g, embed_ref, head_ref, gain_ref = refs[:9]
    refs = refs[9:]
    outs = [refs[4 * i : 4 + 4 * i] for i in range(6)]
    bufs = [refs[24 + 4 * i : 28 + 4 * i] for i in range(6)]
    states = [refs[48 + 3 * i : 51 + 3 * i] for i in range(6)]
    sems, in_sems = refs[66:68]
    order = (0, 2, 3, 4, 1, 5)

    def fetches(i):
        return [
            pltpu.make_async_copy(source, state, in_sems.at[i, k])
            for k, (source, state) in enumerate(zip(sources[i], states[i]))
        ]

    for i in order:
        for copy in fetches(i):
            copy.start()

    def arrive(i):
        for copy in fetches(i):
            copy.wait()

    scale = scale_ref[0]
    even = c_ref[0] == 0

    def pair(keep, got):
        return jnp.where(even, keep, got) * scale, jnp.where(even, got, keep) * scale

    def step(i, at, grad):
        master_ref, first_ref, second_ref = states[i]
        rate = RATE_GAIN if i == 5 else RATE_MATRIX
        decay = 0.0 if i == 5 else DECAY_RATE
        master = master_ref[at]
        first_new = 0.5 * first_ref[at] + 0.5 * grad
        second_new = 0.5 * second_ref[at] + 0.5 * grad * grad
        master_new = master - rate * (
            first_new * (1.0 / correct) / (jnp.sqrt(second_new * (1.0 / correct)) + ADAM_EPS)
            + decay * master
        )
        for buf, value in zip(bufs[i], (master_new, first_new, second_new, master_new.astype(BF))):
            buf[at] = value

    def copies(i):
        return [
            pltpu.make_async_copy(buf, out, sems.at[i, k])
            for k, (buf, out) in enumerate(zip(bufs[i], outs[i]))
        ]

    def send(i):
        for copy in copies(i):
            copy.start()

    every = slice(None)
    arrive(0)
    lanes = states[0][0].shape[2] // 2
    for j in range(3):
        cut = slice(j * lanes, (j + 1) * lanes)
        for k, grad in enumerate(pair(attn_k[:, cut], attn_g[:, cut])):
            step(0, (j, every, slice(k * lanes, (k + 1) * lanes)), grad)
    send(0)
    arrive(2)
    size = states[2][0].shape[1] // 2
    for k, grad in enumerate(pair(up_k[...], up_g[...])):
        step(2, (every, slice(k * size, (k + 1) * size)), grad)
    send(2)
    arrive(3)
    size = states[3][0].shape[0] // 2
    for k, grad in enumerate(pair(down_k[...], down_g[...])):
        step(3, (slice(k * size, (k + 1) * size), every), grad.T)
    send(3)
    arrive(4)
    vocab = states[4][0].shape[2]
    step(4, (0, every, every), embed_ref[:, 0:vocab] * scale)
    step(4, (1, every, every), head_ref[:, 0:vocab] * scale)
    send(4)
    arrive(1)
    size = states[1][0].shape[0] // 2
    cut = slice(3 * lanes, attn_k.shape[1])
    for k, grad in enumerate(pair(attn_k[:, cut], attn_g[:, cut])):
        step(1, (slice(k * size, (k + 1) * size), every), grad.T)
    send(1)
    arrive(5)
    step(5, (every, every), gain_ref[...] * scale)
    send(5)
    for i in range(6):
        for copy in copies(i):
            copy.wait()


def adam(scale, c_index, states, grads):
    shapes = []
    for group in states:
        shapes += [jax.ShapeDtypeStruct(group[0].shape, t) for t in (F32, F32, F32, BF)]
    args = [v for group in states for v in group] + list(grads)
    vmem, smem = pl.BlockSpec(memory_space=pltpu.VMEM), pl.BlockSpec(memory_space=pltpu.SMEM)
    hbm = pl.BlockSpec(memory_space=pl.ANY)
    return pl.pallas_call(
        adam_kernel,
        in_specs=[smem, smem] + [hbm] * 18 + [vmem] * len(grads),
        out_specs=[hbm] * len(shapes),
        out_shape=shapes,
        scratch_shapes=[pltpu.VMEM(s.shape, s.dtype) for s in shapes]
        + [pltpu.VMEM(v.shape, v.dtype) for v in args[:18]]
        + [pltpu.SemaphoreType.DMA((6, 4)), pltpu.SemaphoreType.DMA((6, 3))],
        compiler_params=pltpu.CompilerParams(vmem_limit_bytes=2 * VMEM_BYTES),
        cost_estimate=cheap(),
        name="adam",
    )(scale, c_index, *args)


def body(
    codes,
    doc_lengths,
    loss_mask,
    qkv_master,
    qkv_first,
    qkv_second,
    out_master,
    out_first,
    out_second,
    up_master,
    up_first,
    up_second,
    down_master,
    down_first,
    down_second,
    table_master,
    table_first,
    table_second,
    gain_master,
    gain_first,
    gain_second,
):
    place = Place()
    nz, ny, nb = place.nz, place.ny, len(place.blocks)
    c, z = place.c, place.z
    feat = qkv_master.shape[0]
    width = feat * place.dp
    total_rows = codes.shape[1]
    half_rows = total_rows // 2
    vocab = table_master.shape[1]
    thin = table_master.shape[2]

    joined = jnp.concatenate([codes, loss_mask, doc_lengths], 1)
    other = place.swap_c(joined)
    four = place.in_order(joined, other, 0)
    row = lax.dynamic_index_in_dim(four, z, 0, keepdims=False)
    codes_row = row[:total_rows]
    mask_row = row[total_rows : 2 * total_rows]
    lengths_row = row[2 * total_rows :]
    doc_ids, starts, local_pos = doc_layout(lengths_row, total_rows)
    targets = next_codes(codes_row, doc_ids, vocab - 1)
    first_row = c * half_rows
    my_codes = lax.dynamic_slice_in_dim(codes_row, first_row, half_rows, 0)
    my_local = lax.dynamic_slice_in_dim(local_pos, first_row, half_rows, 0)
    my_targets = lax.dynamic_slice_in_dim(targets, first_row, half_rows, 0)
    my_mask = lax.dynamic_slice_in_dim(mask_row, first_row, half_rows, 0).astype(F32)
    c_index = jnp.reshape(c, (1,)).astype(jnp.int32)
    starts_col = starts.reshape(total_rows, 1)

    def halves(matrix, axis):
        size = matrix.shape[axis] // 2
        keep = lax.dynamic_slice_in_dim(matrix, c * size, size, axis)
        send = lax.dynamic_slice_in_dim(matrix, (1 - c) * size, size, axis)
        return keep, send

    cols = -(-(vocab + 3) // 128) * 128
    table_t = jnp.swapaxes(table_master.astype(BF), 1, 2)
    embed_p = jnp.concatenate(
        [table_t[0], gain_master.astype(BF).T, jnp.zeros((thin, cols - vocab - 3), BF)], 1
    )
    head_p = jnp.concatenate([table_t[1], jnp.zeros((thin, cols - vocab), BF)], 1)
    slots = Slots()
    g_embed, g_head = GatherTable(place, embed_p), Gather(place, head_p, 0)

    qkv_b, out_b, up_b, down_b = (
        v.astype(BF) for v in (qkv_master, out_master, up_master, down_master)
    )
    qkv_k, qkv_s = (v.reshape(feat, -1) for v in halves(qkv_b, 2))
    out_k, out_s = (v.T for v in halves(out_b, 0))
    up_k, up_s = halves(up_b, 1)
    down_k, down_s = (v.T for v in halves(down_b, 0))
    units = [v.shape[1] for v in (qkv_k, out_k, up_k, down_k)]
    keep = jnp.concatenate([qkv_k, out_k, up_k, down_k], 1)
    send = jnp.concatenate([qkv_s, out_s, up_s, down_s], 1)
    recv = place.swap_c(send)
    chip = place.in_order(keep, recv, 0)
    edges = [sum(units[:i]) for i in range(5)]
    g_attn = Gather(place, chip[:, : edges[2]], 1, [(0, units[0]), (units[0], edges[2])])
    g_up = Gather(place, chip[:, edges[2] : edges[3]], 1)
    g_down = Gather(place, chip[:, edges[3] :], 1)

    block = jnp.asarray([k for k, _ in place.blocks], jnp.int32)
    block_x = jnp.asarray([k for _, k in place.blocks], jnp.int32)
    chip_at = ((place.y + block) % ny) * 2 + (place.x ^ block_x)
    feature = (
        chip_at[:, None] * (2 * feat) + jnp.arange(2 * feat, dtype=jnp.int32)[None, :]
    ).reshape(width)
    freqs = jnp.exp((feature // 2).astype(F32) * (-2.0 * math.log(10000.0) / width))
    local_c = Cell(my_local)
    fence(local_c, g_attn.wide)
    angles = local_c.v.astype(F32)[:, None] * freqs[None, :]
    coded = Cell(jnp.where((feature % 2 == 0)[None, :], jnp.sin(angles), jnp.cos(angles)))

    def branch(lefts, gather, span):
        theirs = back(lefts, gather, span, half_rows, half_rows, BF)
        got = place.swap_c(theirs)
        return back(lefts, gather, span, 0, half_rows, F32), got

    def table(gather):
        a, b = (jnp.stack(v) for v in gather.pieces())
        mine = jnp.concatenate([a, b], 1).reshape(nb, 1, nz * thin, cols)
        return place.in_order(mine, place.swap_c(mine), 1).reshape(width, cols)

    def code_rows(half):
        own = lax.dynamic_slice_in_dim(codes_row, half * half_rows, half_rows, 0)
        gain_codes = vocab + jnp.arange(16, dtype=jnp.int32)
        return jnp.concatenate([own, jnp.where(gain_codes < vocab + 3, gain_codes, -1)])[:, None]

    codes_c = cells(code_rows(c), code_rows(1 - c))
    g_embed.over_z()
    g_attn.over_z()
    fence(g_attn.parts, coded)
    slots.slot([g_attn.near, g_embed.around])
    g_up.over_z(g_attn.parts)
    g_down.over_z(g_up.parts)
    slots.slot([g_up.near, g_attn.far])
    g_head.over_z(g_down.parts)
    found, found_other = lookup(codes_c[0].v, codes_c[1].v, g_embed)
    start, attn_m, gains = start_norm(nb, c_index, found, place.swap_c(found_other), coded.v)
    gains = [gains[i : i + 1] for i in range(3)]
    one_hot = (my_codes[:, None] == jnp.arange(cols, dtype=jnp.int32)[None, :]).astype(BF)
    attn_c, other_c = cells(attn_m, place.swap_c(attn_m))

    slots.slot([g_down.near, g_up.far], attn_c, other_c, g_head.parts)
    span_qkv = (0, nz // 2 * units[0])
    span_out = (span_qkv[1], nz // 2 * edges[2])
    span_up, span_down = (0, nz // 2 * units[2]), (0, nz // 2 * units[3])
    attn_in, qkv, _ = across(attn_c.v, other_c.v, g_attn, span_qkv)
    mixed, lse = zip(*(attention(c_index, starts_col, v) for v in qkv))
    theirs_c = Cell(back(mixed, g_attn, span_out, half_rows, half_rows, BF))
    mine_c = Cell(back(mixed, g_attn, span_out, 0, half_rows, F32))

    slots.slot([g_head.near, g_down.far], theirs_c, mine_c)
    middle, ffn_m = norm([start, mine_c.v, place.swap_c(theirs_c.v)], gains[1])
    ffn_in, hidden, slope = across(ffn_m, place.swap_c(ffn_m), g_up, span_up, "gelu")
    hidden_c = cells(*hidden)
    slots.slot([g_head.far], *hidden_c)
    hidden = [v.v for v in hidden_c]
    final, features = norm([middle, *branch(hidden, g_down, span_down)], gains[2])
    a, b = (jnp.stack(v) for v in g_head.pieces())
    mine = jnp.concatenate([a, b], 1).reshape(nb, 1, nz * thin, cols)
    head_t = place.in_order(mine, place.swap_c(mine), 1).reshape(width, cols)
    logits = dot(features, head_t)
    logits = jnp.where(jnp.arange(cols)[None, :] < vocab, logits, -1e30)
    loss_local, grad_logits = head_loss(logits, my_targets, my_mask)

    slots = Slots()
    cut = 2 * feat

    def matrix_sum(*pairs):
        whole = weight_grads(place, *pairs)
        groups, start_at = [], 0
        for _, rights in pairs:
            size = rights[0].shape[1] // (nz // 2)
            groups.append((start_at, start_at + size))
            start_at += size
        return Reduce(place, whole, 1, groups)

    def table_sum(left, right, extra=None):
        def by_c(values):
            size = nz * thin
            even, odd = (
                jnp.concatenate([values[..., (2 * i + k) * size : (2 * i + k + 1) * size] for i in range(nb)], -1)
                for k in (0, 1)
            )
            return jnp.where(c == 0, even, odd), jnp.where(c == 0, odd, even)

        left_k, left_s = by_c(left)
        own = dot(left_k, right, TN)
        sent = dot(left_s, right, TN)
        if extra is not None:
            extra_k, extra_s = (
                jnp.pad(v.T, ((0, 0), (vocab, cols - vocab - extra.shape[0]))) for v in by_c(extra)
            )
            own, sent = own + extra_k, sent + extra_s
        got = place.swap_c(sent.astype(BF))
        chip_sum = (own + got.astype(F32)).astype(BF).reshape(nb, 2, nz // 2 * thin, cols)
        return Reduce(place, [chip_sum[:, 0], chip_sum[:, 1]], 0)

    r_head = table_sum(features, grad_logits)
    grad_feat = dot(grad_logits, head_t, NT)
    grad_final, grad_down, gain_three = norm_back([grad_feat], [], final, gains[2])
    grad_down_c, other_c = cells(grad_down, place.swap_c(grad_down))
    slots.slot([r_head.near], grad_down_c, other_c)
    grad_down, other = grad_down_c.v, other_c.v
    r_down = matrix_sum((jnp.concatenate([grad_down, other], 0), hidden))

    grad_down_c, other_c = cells(grad_down, other)
    slots.slot([r_down.near, r_head.far], grad_down_c, other_c)
    _, grad_up, _ = across(grad_down_c.v, other_c.v, g_down, span_down, "slope", slope)
    theirs_c = Cell(back(grad_up, g_up, span_up, half_rows, half_rows, BF))
    mine_c = Cell(back(grad_up, g_up, span_up, 0, half_rows, F32))
    r_up = matrix_sum((ffn_in, grad_up))

    slots.slot([r_up.near, r_down.far], theirs_c, mine_c)
    grad_mid, grad_out, gain_two = norm_back(
        [mine_c.v, place.swap_c(theirs_c.v)], [grad_final], middle, gains[1]
    )
    grad_out, grad_mixed, _ = across(grad_out, place.swap_c(grad_out), g_attn, span_out)
    grad_qkv = [
        attention_back(c_index, starts_col, q, o, g, ls)
        for q, o, g, ls in zip(qkv, mixed, grad_mixed, lse)
    ]
    r_attn = matrix_sum((attn_in, grad_qkv), (grad_out, mixed))
    theirs_c = Cell(back(grad_qkv, g_attn, span_qkv, half_rows, half_rows, BF))
    mine_c = Cell(back(grad_qkv, g_attn, span_qkv, 0, half_rows, F32))

    slots.slot([r_attn.near, r_up.far], theirs_c, mine_c)
    r_down.over_z()
    grad_start, _, gain_one = norm_back(
        [mine_c.v, place.swap_c(theirs_c.v)], [grad_mid], start, gains[0]
    )
    gain_grad = jnp.concatenate([gain_one, gain_two, gain_three], 0)
    r_embed = table_sum((grad_start * math.sqrt(width)).astype(BF), one_hot, gain_grad)

    slots.slot([r_attn.far, r_embed.near])
    r_up.over_z(r_down.got)
    slots.slot([r_embed.far])
    r_head.over_z(slots.flight[0])
    r_attn.over_z(r_up.got)
    r_embed.over_z(r_up.got)

    def shards(total):
        keep_g, send_g = halves(total, 0)
        return keep_g, place.swap_c(send_g)

    head_sum, down_sum, up_sum = r_head.result(), r_down.result(), r_up.result()
    down_k, down_g = shards(down_sum)
    up_k, up_g = shards(up_sum)
    attn_sum = r_attn.result()
    attn_k, attn_g = shards(attn_sum)
    embed_sum = r_embed.result()
    squares = sum(
        jnp.sum(v * v) for v in (head_sum, down_sum, up_sum, attn_sum, embed_sum)
    )
    stats = jnp.stack([loss_local, jnp.sum(my_mask), squares])
    stats = place.total(stats)
    loss_all, count_all = stats[0], stats[1]
    norm_all = jnp.sqrt(stats[2] / (count_all * count_all))
    factor = jnp.minimum(1.0, CLIP_NORM / (norm_all + 1e-06))
    scale = jnp.reshape(factor / count_all, (1,))
    states = (
        [jnp.swapaxes(v, 0, 1) for v in (qkv_master, qkv_first, qkv_second)],
        (out_master, out_first, out_second),
        (up_master, up_first, up_second),
        (down_master, down_first, down_second),
        [jnp.swapaxes(v, 1, 2) for v in (table_master, table_first, table_second)],
        (gain_master, gain_first, gain_second),
    )
    gain_sum = embed_sum[:, vocab : vocab + 3].T
    grads = (attn_k, attn_g, up_k, up_g, down_k, down_g, embed_sum, head_sum, gain_sum)
    new = list(adam(scale, c_index, states, grads))
    new[0:4] = [jnp.swapaxes(v, 0, 1) for v in new[0:4]]
    new[16:20] = [jnp.swapaxes(v, 1, 2) for v in new[16:20]]
    return tuple(new) + (loss_all, count_all, norm_all)


def solution(mesh):
    rows, cols = P("dp", None, "tensor"), P("tensor", "dp")
    plain, both, gain = P("dp", "tensor"), P(None, None, ("dp", "tensor")), P(None, ("dp", "tensor"))
    kinds = (rows, cols, plain, cols, both, gain)
    in_specs = (P("dp", None),) * 3 + tuple(k for k in kinds for _ in range(3))
    out_specs = tuple(k for k in kinds for _ in range(4)) + (P(),) * 3
    return jax.shard_map(body, mesh=mesh, in_specs=in_specs, out_specs=out_specs, check_vma=False)
```

```python
import functools
import math

import jax
import jax.numpy as jnp
from jax import lax
from jax.experimental import pallas as pl
from jax.experimental.pallas import tpu as pltpu
from jax.sharding import PartitionSpec as P

HEAD = 64
STEP = 5

RATE_MATRIX = 0.03
RATE_GAIN = 0.25
DECAY_RATE = 0.01
CLIP_NORM = 0.002
NORM_EPS = 1e-05
ADAM_EPS = 1e-08

BF = jnp.bfloat16
F32 = jnp.float32
LOG2E = math.log2(math.e)
NN = (((1,), (0,)), ((), ()))
NT = (((1,), (1,)), ((), ()))
TN = (((0,), (0,)), ((), ()))
VMEM_BYTES = 28 * 1024 * 1024
SMALL_VMEM = 24 * 1024 * 1024


def dot(left, right, dims=NN):
    return lax.dot_general(left, right, dims, preferred_element_type=F32)


def barrier(*values):
    return lax.optimization_barrier(values)


class Place:
    def __init__(self):
        self.dp = lax.axis_size("dp")
        self.nz = lax.axis_size("tensor")
        self.ny = self.dp // 4
        index = lax.axis_index("dp")
        self.z = lax.axis_index("tensor")
        self.c = index % 2
        self.x = (index // 2) % 2
        self.y = index // 4
        self.blocks = [(0, 0), (0, 1)]
        self.blocks += [(k, 1) for k in range(1, self.ny)]
        self.blocks += [(k, 0) for k in range(1, self.ny)]

    def at(self, ky, kx):
        return self.blocks.index((ky, kx))

    def swap_c(self, value):
        return lax.ppermute(value, "dp", [(i, i ^ 1) for i in range(self.dp)])

    def swap_x(self, value):
        return lax.ppermute(value, "dp", [(i, i ^ 2) for i in range(self.dp)])

    def from_y(self, value, k):
        n = self.dp
        return lax.ppermute(value, "dp", [((i + 4 * k) % n, i) for i in range(n)])

    def to_y(self, value, k):
        n = self.dp
        return lax.ppermute(value, "dp", [(i, (i + 4 * k) % n) for i in range(n)])

    def from_z(self, value, k):
        n = self.nz
        return lax.ppermute(value, "tensor", [((i + k) % n, i) for i in range(n)])

    def to_z(self, value, k):
        n = self.nz
        return lax.ppermute(value, "tensor", [(i, (i + k) % n) for i in range(n)])

    def all_z(self, value):
        return lax.all_to_all(value, "tensor", 0, 0)

    def from_block(self, value, block):
        (ky, kx), n = block, self.dp
        return lax.ppermute(value, "dp", [(((i ^ (2 * kx)) + 4 * ky) % n, i) for i in range(n)])

    def total(self, value):
        value = value + self.swap_c(value)
        n = self.dp
        around = [
            lax.ppermute(value, "dp", [(((i ^ (2 * kx)) + 4 * ky) % n, i) for i in range(n)])
            for ky, kx in self.blocks[1:]
        ]
        value = value + sum(around)
        return value + sum(self.from_z(value, k) for k in range(1, self.nz))

    def in_order(self, mine, other, axis):
        first = jnp.where(self.c == 0, mine, other)
        last = jnp.where(self.c == 0, other, mine)
        return jnp.concatenate([first, last], axis)


class Cell:
    def __init__(self, value):
        self.v = value


def cells(*values):
    return [Cell(v) for v in values]


def fence(*held):
    held = list(dict.fromkeys(held))
    for cell, value in zip(held, barrier(*[c.v for c in held])):
        cell.v = value


class Slots:
    def __init__(self):
        self.flight = []

    def slot(self, stages, *also, wait=True):
        plans = [stage() for stage in stages]
        sends = [s for plan, _ in plans for s in plan]
        fence(*(self.flight if wait else ()), *[c for _, c in sends], *also)
        out = [Cell(send(c.v)) for send, c in sends]
        self.flight = out if wait else self.flight + out
        at = 0
        for plan, take in plans:
            take(out[at : at + len(plan)])
            at += len(plan)


class Gather:
    def __init__(self, place, own, axis, groups=None):
        self.place, self.own, self.axis, self.groups = place, Cell(own), axis, groups
        self.wide = Cell(jnp.broadcast_to(own[None], (place.nz,) + own.shape))
        self.ks = range(1, place.ny)

    def over_z(self, *after):
        fence(self.wide, *after)
        self.parts = Cell(self.place.all_z(self.wide.v))

    def near(self):
        place, half = self.place, self.place.nz // 2
        parts, groups = self.parts.v, self.groups or [(0, self.own.v.shape[1])]
        self.both = Cell(
            jnp.stack(
                [
                    jnp.concatenate(
                        [parts[i][:, g0:g1] for g0, g1 in groups for i in range(lo, lo + half)],
                        self.axis,
                    )
                    for lo in (0, half)
                ]
            )
        )

        def take(out):
            self.by_x, self.by_y = out[0], out[1:]

        plan = [(place.swap_x, self.both)]
        return plan + [(functools.partial(place.from_y, k=k), self.both) for k in self.ks], take

    def far(self):
        place = self.place

        def take(out):
            self.far_a, self.far_b = out[: place.ny - 1], out[place.ny - 1 :]

        plan = [(lambda v: place.swap_x(v[0]), v) for v in self.by_y]
        return plan + [(lambda v, k=k: place.from_y(v[1], k), self.by_x) for k in self.ks], take

    def pieces(self):
        out = []
        for half, far in ((0, self.far_a), (1, self.far_b)):
            out.append(
                [self.both.v[half], self.by_x.v[half]]
                + [v.v for v in far]
                + [v.v[half] for v in self.by_y]
            )
        return out

    def arrays(self):
        cells = [self.both, self.by_x, *self.far_a, *self.far_b, *self.by_y]
        return [c.v for c in cells]


class Reduce:
    def __init__(self, place, whole, axis, groups=None):
        self.place, self.whole, self.axis, self.groups = place, whole, axis, groups
        self.ks = range(1, place.ny)

    def near(self):
        place = self.place
        a, b = self.whole

        def take(out):
            self.got_a, self.got_b = out[0], out[1:]

        plan = [(place.swap_x, Cell(a[1 : 1 + place.ny]))]
        for k in self.ks:
            if place.ny == 2:
                sent = b[2:4]
            else:
                sent = jnp.stack([b[place.at(k, 1)], b[place.at(k, 0)]])
            plan.append((functools.partial(place.to_y, k=k), Cell(sent)))
        return plan, take

    def far(self):
        place = self.place
        a, b = self.whole

        def take(out):
            self.far_a, self.far_b = out[:-1], out[-1]

        def along(got, k):
            sent = a[place.at(k, 0)].astype(F32) + got[k].astype(F32)
            return place.to_y(sent.astype(BF), k)

        def across(first):
            sent = b[1].astype(F32) + first[0].astype(F32)
            for other in self.got_b[1:]:
                sent = sent + other.v[0].astype(F32)
            return place.swap_x(sent.astype(BF))

        plan = [(functools.partial(along, k=k), self.got_a) for k in self.ks]
        return plan + [(across, self.got_b[0])], take

    def over_z(self, *after):
        place, half = self.place, self.place.nz // 2
        a, b = self.whole
        own_a = a[0].astype(F32) + self.got_a.v[0].astype(F32) + sum(v.v.astype(F32) for v in self.far_a)
        own_b = (
            b[0].astype(F32) + sum(v.v[1].astype(F32) for v in self.got_b) + self.far_b.v.astype(F32)
        )
        if self.axis == 0:
            chunks = jnp.split(own_a, half, 0) + jnp.split(own_b, half, 0)
        else:
            chunks = []
            for own in (own_a, own_b):
                parts = [jnp.split(own[:, half * g0 : half * g1], half, 1) for g0, g1 in self.groups]
                chunks += [jnp.concatenate(v, 1) for v in zip(*parts)]
        sent = Cell(jnp.stack([v.astype(BF) for v in chunks]))
        fence(sent, *after)
        if self.axis == 0:
            pieces = [
                lax.dynamic_index_in_dim(sent.v, (place.z + k) % place.nz, 0, keepdims=False)
                for k in range(place.nz)
            ]
            moved = [place.to_z(pieces[k], k) for k in range(1, place.nz)]
            self.got = Cell(jnp.stack(pieces[:1] + moved))
        else:
            self.got = Cell(place.all_z(sent.v))

    def result(self):
        return jnp.sum(self.got.v.astype(F32), 0)


class GatherTable:
    def __init__(self, place, own):
        self.place, self.own = place, own

    def over_z(self):
        place, own = self.place, self.own
        parts = [own] + [place.from_z(own, k) for k in range(1, place.nz)]
        parts = jnp.roll(jnp.stack(parts), place.z, 0)
        self.parts = Cell(parts.reshape(-1, own.shape[1]))

    def around(self):
        place = self.place

        def take(out):
            self.others = out

        return [
            (functools.partial(place.from_block, block=block), self.parts) for block in place.blocks[1:]
        ], take

    def arrays(self):
        return [c.v for c in [self.parts] + self.others]


def forward_kernel(c_ref, start_ref, qkv_ref, o_ref, lse_ref, k_s, v_s):
    c = c_ref[0]
    half = qkv_ref.shape[1]
    total = 2 * half
    block = min(256, half)
    per_half = half // block
    scale = HEAD ** (-0.5) * LOG2E
    for b in range(2):
        k_s[b * half : (b + 1) * half] = qkv_ref[b ^ c, :, 128:256]
        v_s[b * half : (b + 1) * half] = qkv_ref[b ^ c, :, 256:384]
    lane = lax.broadcasted_iota(jnp.int32, (block, 128), 1)
    for qb in range(total // block):
        rel = (qb // per_half) ^ c
        r0 = (qb % per_half) * block
        n = (qb + 1) * block
        q = qkv_ref[rel, r0 : r0 + block, 0:128]
        row = qb * block + lax.broadcasted_iota(jnp.int32, (block, n), 0)
        col = lax.broadcasted_iota(jnp.int32, (block, n), 1)
        start = start_ref[qb * block : (qb + 1) * block, 0:1]
        allowed = (col >= start) & (col <= row)
        outs = []
        for h in range(2):
            qh = jnp.where((lane >= 64) == (h == 1), q, jnp.zeros_like(q))
            s = dot(qh, k_s[0:n], NT)
            s = jnp.where(allowed, s, -1e30)
            top = jnp.max(s, -1, keepdims=True)
            p = jnp.exp2((s - top) * scale)
            total_p = jnp.sum(p, -1, keepdims=True)
            outs.append(dot(p.astype(BF), v_s[0:n]) / total_p)
            lse = top * scale + jnp.log2(total_p)
            lse_ref[0, qb * block : (qb + 1) * block, h * 64 : (h + 1) * 64] = jnp.broadcast_to(
                lse, (block, 64)
            )
        o_ref[rel, r0 : r0 + block, :] = jnp.where(lane < 64, outs[0], outs[1]).astype(BF)


def backward_kernel(c_ref, start_ref, qkv_ref, o_ref, go_ref, lse_ref, out_ref, k_s, v_s, gk_s, gv_s):
    c = c_ref[0]
    half = qkv_ref.shape[1]
    total = 2 * half
    block = min(256, half)
    per_half = half // block
    scale = HEAD ** (-0.5)
    for b in range(2):
        k_s[b * half : (b + 1) * half] = qkv_ref[b ^ c, :, 128:256]
        v_s[b * half : (b + 1) * half] = qkv_ref[b ^ c, :, 256:384]
    lane = lax.broadcasted_iota(jnp.int32, (block, 128), 1)
    for step, qb in enumerate(reversed(range(total // block))):
        rel = (qb // per_half) ^ c
        r0 = (qb % per_half) * block
        n = (qb + 1) * block
        q = qkv_ref[rel, r0 : r0 + block, 0:128]
        go = go_ref[rel, r0 : r0 + block, :]
        o = o_ref[rel, r0 : r0 + block, :]
        row = qb * block + lax.broadcasted_iota(jnp.int32, (block, n), 0)
        col = lax.broadcasted_iota(jnp.int32, (block, n), 1)
        start = start_ref[qb * block : (qb + 1) * block, 0:1]
        allowed = (col >= start) & (col <= row)
        both = go.astype(F32) * o.astype(F32)
        gq = None
        for h in range(2):
            mine = (lane >= 64) == (h == 1)
            qh = jnp.where(mine, q, jnp.zeros_like(q))
            gh = jnp.where(mine, go, jnp.zeros_like(go))
            s = dot(qh, k_s[0:n], NT)
            lse = lse_ref[0, qb * block : (qb + 1) * block, h * 64 : h * 64 + 1]
            p = jnp.where(allowed, jnp.exp2(jnp.minimum(s * (scale * LOG2E) - lse, 1.0)), 0.0)
            gp = dot(gh, v_s[0:n], NT)
            inner = jnp.sum(jnp.where(mine, both, 0.0), -1, keepdims=True)
            gs = (p * (gp - inner)).astype(BF)
            pb = p.astype(BF)
            gqh = dot(gs, k_s[0:n])
            gq = gqh if gq is None else jnp.where(lane < 64, gq, gqh)
            gk = dot(gs, qh, TN)
            gv = dot(pb, gh, TN)
            if step == 0 and h == 0:
                gk_s[0:n] = gk
                gv_s[0:n] = gv
            else:
                gk_s[0:n] += gk
                gv_s[0:n] += gv
        out_ref[rel, r0 : r0 + block, 0:128] = (gq * scale).astype(BF)
    for b in range(2):
        out_ref[b ^ c, :, 128:256] = (gk_s[b * half : (b + 1) * half] * scale).astype(BF)
        out_ref[b ^ c, :, 256:384] = gv_s[b * half : (b + 1) * half].astype(BF)


def attention(c_index, starts, qkv):
    rows, cols = qkv.shape
    half, pairs = rows // 2, cols // 384
    smem = pl.BlockSpec(memory_space=pltpu.SMEM)
    out, lse = pl.pallas_call(
        forward_kernel,
        grid=(pairs,),
        in_specs=[
            smem,
            pl.BlockSpec((rows, 1), lambda j: (0, 0)),
            pl.BlockSpec((2, half, 384), lambda j: (0, 0, j)),
        ],
        out_specs=[
            pl.BlockSpec((2, half, 128), lambda j: (0, 0, j)),
            pl.BlockSpec((1, rows, 128), lambda j: (j, 0, 0)),
        ],
        out_shape=[
            jax.ShapeDtypeStruct((2, half, pairs * 128), BF),
            jax.ShapeDtypeStruct((pairs, rows, 128), F32),
        ],
        scratch_shapes=[pltpu.VMEM((rows, 128), BF), pltpu.VMEM((rows, 128), BF)],
        compiler_params=pltpu.CompilerParams(vmem_limit_bytes=VMEM_BYTES),
        cost_estimate=pl.CostEstimate(
            flops=1, bytes_accessed=1, transcendentals=0
        ),
        name="attend",
    )(c_index, starts, qkv.reshape(2, half, cols))
    return out.reshape(rows, pairs * 128), lse


def attention_back(c_index, starts, qkv, out, grad, lse):
    rows, cols = qkv.shape
    half, pairs = rows // 2, cols // 384
    smem = pl.BlockSpec(memory_space=pltpu.SMEM)
    wide = pl.BlockSpec((2, half, 384), lambda j: (0, 0, j))
    thin = pl.BlockSpec((2, half, 128), lambda j: (0, 0, j))
    result = pl.pallas_call(
        backward_kernel,
        grid=(pairs,),
        in_specs=[
            smem,
            pl.BlockSpec((rows, 1), lambda j: (0, 0)),
            wide,
            thin,
            thin,
            pl.BlockSpec((1, rows, 128), lambda j: (j, 0, 0)),
        ],
        out_specs=wide,
        out_shape=jax.ShapeDtypeStruct((2, half, cols), BF),
        scratch_shapes=[
            pltpu.VMEM((rows, 128), BF),
            pltpu.VMEM((rows, 128), BF),
            pltpu.VMEM((rows, 128), F32),
            pltpu.VMEM((rows, 128), F32),
        ],
        compiler_params=pltpu.CompilerParams(vmem_limit_bytes=VMEM_BYTES),
        cost_estimate=pl.CostEstimate(
            flops=1, bytes_accessed=1, transcendentals=0
        ),
        name="attend_back",
    )(
        c_index,
        starts,
        qkv.reshape(2, half, cols),
        out.reshape(2, half, pairs * 128),
        grad.reshape(2, half, pairs * 128),
        lse,
    )
    return result.reshape(rows, cols)


def cheap():
    return pl.CostEstimate(flops=1, bytes_accessed=1, transcendentals=0)


def call(kernel, args, shapes, scratch=(), name=None):
    vmem = pl.BlockSpec(memory_space=pltpu.VMEM)
    return pl.pallas_call(
        kernel,
        in_specs=[vmem] * len(args),
        out_specs=[vmem] * len(shapes),
        out_shape=shapes,
        scratch_shapes=list(scratch),
        compiler_params=pltpu.CompilerParams(vmem_limit_bytes=SMALL_VMEM),
        cost_estimate=cheap(),
        name=name,
    )(*args)


def piece_at(refs, blocks, half, i):
    far = (blocks - 2) // 2
    if i < 2:
        return refs[i].at[half]
    if i < 2 + far:
        return refs[i + half * far]
    return refs[i + far].at[half]


def gelu_parts(value):
    phi = 0.5 * (1.0 + lax.erf(value * (0.5**0.5)))
    slope = phi + value * (jnp.exp(-0.5 * value * value) * (1.0 / math.sqrt(2.0 * math.pi)))
    return value * phi, slope


def across_kernel(blocks, count, lo, hi, kind, *refs):
    mine_ref, theirs_ref = refs[:2]
    weights = refs[2 : 2 + count]
    refs = refs[2 + count :]
    slopes = ()
    if kind == "slope":
        slopes, refs = refs[:2], refs[2:]
    joined_ref, refs = refs[0], refs[1:]
    outs, w_s = refs[:-1], refs[-1]
    rows = mine_ref.shape[0]
    tile = min(512, rows)
    size = w_s.shape[1] // blocks
    for half in range(2):
        for i in range(blocks):
            w_s[half, i * size : (i + 1) * size] = piece_at(weights, blocks, half, i)[:, lo:hi]
    for base, source in ((0, mine_ref), (rows, theirs_ref)):

        @pl.loop(0, rows // tile)
        def _(step):
            r = pl.multiple_of(step * tile, tile)
            at = pl.ds(pl.multiple_of(base + step * tile, tile), tile)
            left = source[pl.ds(r, tile), :]
            joined_ref[at, :] = left
            for half in range(2):
                value = dot(left, w_s[half])
                if kind == "gelu":
                    value, slope = gelu_parts(value)
                    outs[2 + half][at, :] = slope.astype(BF)
                elif kind == "slope":
                    value = value * slopes[half][at, :].astype(F32)
                outs[half][at, :] = value.astype(BF)


def across(mine, theirs, gather, span, kind="plain", slopes=()):
    arrays = gather.arrays()
    blocks = len(gather.place.blocks)
    lo, hi = span
    rows, width = mine.shape
    units = hi - lo
    count = 4 if kind == "gelu" else 2
    out = call(
        functools.partial(across_kernel, blocks, len(arrays), lo, hi, kind),
        [mine, theirs, *arrays, *slopes],
        [jax.ShapeDtypeStruct((2 * rows, width), BF)]
        + [jax.ShapeDtypeStruct((2 * rows, units), BF)] * count,
        [pltpu.VMEM((2, width, units), BF)],
        "across_" + kind,
    )
    return out[0], list(out[1:3]), list(out[3:])


def grads_kernel(blocks, sizes, *refs):
    pairs = len(sizes)
    inputs, outs = refs[: 3 * pairs], refs[3 * pairs :]
    cut = inputs[0].shape[1] // blocks
    at = 0
    for p, size in enumerate(sizes):
        left_ref, rights = inputs[3 * p], inputs[3 * p + 1 : 3 * p + 3]
        for i in range(blocks):
            left = left_ref[:, i * cut : (i + 1) * cut]
            for half in range(2):
                value = dot(left, rights[half][...], TN)
                outs[half][i, :, at : at + size] = value.astype(BF)
        at += size


def weight_grads(place, *pairs):
    blocks = len(place.blocks)
    sizes = [rights[0].shape[1] for _, rights in pairs]
    width = pairs[0][0].shape[1]
    args = [v for left, rights in pairs for v in (left, *rights)]
    shape = jax.ShapeDtypeStruct((blocks, width // blocks, sum(sizes)), BF)
    return call(
        functools.partial(grads_kernel, blocks, sizes), args, [shape, shape], (), "grads"
    )


def back_kernel(blocks, count, lo, hi, row0, *refs):
    lefts, weights, out_ref = refs[:2], refs[2 : 2 + count], refs[2 + count]
    rows, width = out_ref.shape
    tile = min(512, rows)
    size = width // blocks

    @pl.loop(0, rows // tile)
    def _(step):
        r = pl.multiple_of(step * tile, tile)
        at = pl.ds(pl.multiple_of(row0 + step * tile, tile), tile)
        left_a, left_b = lefts[0][at, :], lefts[1][at, :]
        for i in range(blocks):
            value = dot(left_a, piece_at(weights, blocks, 0, i)[:, lo:hi], NT)
            value = value + dot(left_b, piece_at(weights, blocks, 1, i)[:, lo:hi], NT)
            out_ref[pl.ds(r, tile), i * size : (i + 1) * size] = value.astype(out_ref.dtype)


def back(lefts, gather, span, row0, rows, dtype):
    arrays = gather.arrays()
    blocks = len(gather.place.blocks)
    width = blocks * arrays[0].shape[1]
    return call(
        functools.partial(back_kernel, blocks, len(arrays), *span, row0),
        [*lefts, *arrays],
        [jax.ShapeDtypeStruct((rows, width), dtype)],
        (),
        "back",
    )[0]


def lookup_kernel(blocks, count, *refs):
    codes_refs, weights, outs = refs[:2], refs[2 : 2 + count], refs[2 + count : -1]
    w_s = refs[-1]
    rows, cols = codes_refs[0].shape[0], weights[0].shape[-1]
    size = weights[0].shape[0]
    for i in range(blocks):
        w_s[i * size : (i + 1) * size] = weights[i][...]
    for codes_ref, out_ref in zip(codes_refs, outs):
        hot = lax.broadcasted_iota(jnp.int32, (rows, cols), 1) == codes_ref[...]
        hot = jnp.where(hot, 1.0, 0.0).astype(BF)
        out_ref[...] = dot(hot, w_s[...], NT).astype(BF)


def lookup(mine, theirs, gather):
    arrays = gather.arrays()
    blocks = len(gather.place.blocks)
    features = blocks * arrays[0].shape[0]
    shape = jax.ShapeDtypeStruct((mine.shape[0], features), BF)
    return call(
        functools.partial(lookup_kernel, blocks, len(arrays)),
        [mine, theirs, *arrays],
        [shape, shape],
        [pltpu.VMEM((features, arrays[0].shape[1]), BF)],
        "lookup",
    )


def start_kernel(blocks, factor, c_ref, mine_ref, got_ref, coded_ref, x_ref, y_ref, gains_ref):
    even = c_ref[0] == 0
    rows, width = x_ref.shape
    tile = min(64, rows)
    size = width // (2 * blocks)

    def both(at):
        mine, got = mine_ref[at, :].astype(F32), got_ref[at, :].astype(F32)
        out = []
        for i in range(blocks):
            a, b = mine[:, i * size : (i + 1) * size], got[:, i * size : (i + 1) * size]
            out += [jnp.where(even, a, b), jnp.where(even, b, a)]
        return jnp.concatenate(out, 1)

    gains_ref[...] = both(slice(rows, mine_ref.shape[0]))

    @pl.loop(0, rows // tile)
    def _(step):
        at = pl.ds(pl.multiple_of(step * tile, tile), tile)
        x = both(at) * factor + coded_ref[at, :]
        x_ref[at, :] = x
        y_ref[at, :] = (row_stats(x)[0] * gains_ref[0:1, :]).astype(BF)


def start_norm(blocks, c_index, mine, got, coded):
    rows, width = coded.shape
    vmem, smem = pl.BlockSpec(memory_space=pltpu.VMEM), pl.BlockSpec(memory_space=pltpu.SMEM)
    return pl.pallas_call(
        functools.partial(start_kernel, blocks, math.sqrt(width)),
        in_specs=[smem, vmem, vmem, vmem],
        out_specs=[vmem] * 3,
        out_shape=[
            jax.ShapeDtypeStruct((rows, width), F32),
            jax.ShapeDtypeStruct((rows, width), BF),
            jax.ShapeDtypeStruct((mine.shape[0] - rows, width), F32),
        ],
        compiler_params=pltpu.CompilerParams(vmem_limit_bytes=SMALL_VMEM),
        cost_estimate=cheap(),
        name="start",
    )(c_index, mine, got, coded)


def row_stats(x):
    centered = x - jnp.mean(x, -1, keepdims=True)
    inverse = lax.rsqrt(jnp.mean(centered * centered, -1, keepdims=True) + NORM_EPS)
    return centered * inverse, inverse


def norm_kernel(terms, *refs):
    parts, gain_ref, x_ref, y_ref = refs[:terms], refs[terms], refs[terms + 1], refs[terms + 2]
    rows = x_ref.shape[0]
    tile = min(64, rows)

    @pl.loop(0, rows // tile)
    def _(step):
        at = pl.ds(pl.multiple_of(step * tile, tile), tile)
        x = parts[0][at, :].astype(F32)
        for part in parts[1:]:
            x = x + part[at, :].astype(F32)
        x_ref[at, :] = x
        y_ref[at, :] = (row_stats(x)[0] * gain_ref[...]).astype(BF)


def norm(parts, gain):
    shape = parts[0].shape
    return call(
        functools.partial(norm_kernel, len(parts)),
        [*parts, gain],
        [jax.ShapeDtypeStruct(shape, F32), jax.ShapeDtypeStruct(shape, BF)],
        (),
        "norm",
    )


def norm_back_kernel(terms, extra, *refs):
    parts, refs = refs[:terms], refs[terms:]
    others, refs = refs[:extra], refs[extra:]
    x_ref, gain_ref, out_ref, low_ref, sum_ref = refs
    rows = x_ref.shape[0]
    tile = min(64, rows)
    sum_ref[...] = jnp.zeros_like(sum_ref)

    @pl.loop(0, rows // tile)
    def _(step):
        at = pl.ds(pl.multiple_of(step * tile, tile), tile)
        grad = parts[0][at, :].astype(F32)
        for part in parts[1:]:
            grad = grad + part[at, :].astype(F32)
        normed, inverse = row_stats(x_ref[at, :])
        scaled = grad * gain_ref[...]
        value = inverse * (
            scaled
            - jnp.mean(scaled, -1, keepdims=True)
            - normed * jnp.mean(scaled * normed, -1, keepdims=True)
        )
        for other in others:
            value = value + other[at, :]
        out_ref[at, :] = value
        low_ref[at, :] = value.astype(BF)
        sum_ref[...] += jnp.sum(grad * normed, 0, keepdims=True)


def norm_back(parts, others, x, gain):
    shape = x.shape
    return call(
        functools.partial(norm_back_kernel, len(parts), len(others)),
        [*parts, *others, x, gain],
        [
            jax.ShapeDtypeStruct(shape, F32),
            jax.ShapeDtypeStruct(shape, BF),
            jax.ShapeDtypeStruct((1, shape[1]), F32),
        ],
        (),
        "norm_back",
    )


def doc_layout(lengths_row, total_rows):
    places = jnp.arange(total_rows, dtype=jnp.int32)
    bound_one = lengths_row[0]
    bound_two = lengths_row[0] + lengths_row[1]
    doc_ids = (places >= bound_one).astype(jnp.int32) + (places >= bound_two).astype(jnp.int32)
    starts = jnp.where(doc_ids == 0, 0, jnp.where(doc_ids == 1, bound_one, bound_two))
    return (doc_ids, starts, places - starts)


def next_codes(codes_row, doc_ids, end_code):
    later = jnp.concatenate([codes_row[1:], jnp.full((1,), end_code, jnp.int32)])
    later_doc = jnp.concatenate([doc_ids[1:], jnp.full((1,), -1, jnp.int32)])
    return jnp.where(later_doc == doc_ids, later, end_code)


def head_loss(logits, targets, weights_row):
    top_score = jnp.max(logits, -1, keepdims=True)
    expo = jnp.exp(logits - top_score)
    totals = jnp.sum(expo, -1, keepdims=True)
    target_hit = jnp.arange(logits.shape[1], dtype=jnp.int32)[None, :] == targets[:, None]
    picked = jnp.sum(jnp.where(target_hit, logits, 0.0), -1)
    loss_value = jnp.sum(weights_row * (top_score[:, 0] + jnp.log(totals[:, 0]) - picked))
    grad_logits = ((expo / totals - target_hit.astype(F32)) * weights_row[:, None]).astype(BF)
    return (loss_value, grad_logits)


def adam_kernel(scale_ref, c_ref, *refs):
    correct = 1.0 - 0.5**STEP
    sources, refs = [refs[3 * i : 3 * i + 3] for i in range(6)], refs[18:]
    attn_k, attn_g, up_k, up_g, down_k, down_g, embed_ref, head_ref, gain_ref = refs[:9]
    refs = refs[9:]
    outs = [refs[4 * i : 4 + 4 * i] for i in range(6)]
    bufs = [refs[24 + 4 * i : 28 + 4 * i] for i in range(6)]
    states = [refs[48 + 3 * i : 51 + 3 * i] for i in range(6)]
    sems, in_sems = refs[66:68]
    order = (0, 2, 3, 4, 1, 5)

    def fetches(i):
        return [
            pltpu.make_async_copy(source, state, in_sems.at[i, k])
            for k, (source, state) in enumerate(zip(sources[i], states[i]))
        ]

    for i in order:
        for copy in fetches(i):
            copy.start()

    def arrive(i):
        for copy in fetches(i):
            copy.wait()

    scale = scale_ref[0]
    even = c_ref[0] == 0

    def pair(keep, got):
        return jnp.where(even, keep, got) * scale, jnp.where(even, got, keep) * scale

    def step(i, at, grad):
        master_ref, first_ref, second_ref = states[i]
        rate = RATE_GAIN if i == 5 else RATE_MATRIX
        decay = 0.0 if i == 5 else DECAY_RATE
        master = master_ref[at]
        first_new = 0.5 * first_ref[at] + 0.5 * grad
        second_new = 0.5 * second_ref[at] + 0.5 * grad * grad
        master_new = master - rate * (
            first_new * (1.0 / correct) / (jnp.sqrt(second_new * (1.0 / correct)) + ADAM_EPS)
            + decay * master
        )
        for buf, value in zip(bufs[i], (master_new, first_new, second_new, master_new.astype(BF))):
            buf[at] = value

    def copies(i):
        return [
            pltpu.make_async_copy(buf, out, sems.at[i, k])
            for k, (buf, out) in enumerate(zip(bufs[i], outs[i]))
        ]

    def send(i):
        for copy in copies(i):
            copy.start()

    every = slice(None)
    arrive(0)
    lanes = states[0][0].shape[2] // 2
    for j in range(3):
        cut = slice(j * lanes, (j + 1) * lanes)
        for k, grad in enumerate(pair(attn_k[:, cut], attn_g[:, cut])):
            step(0, (j, every, slice(k * lanes, (k + 1) * lanes)), grad)
    send(0)
    arrive(2)
    size = states[2][0].shape[1] // 2
    for k, grad in enumerate(pair(up_k[...], up_g[...])):
        step(2, (every, slice(k * size, (k + 1) * size)), grad)
    send(2)
    arrive(3)
    size = states[3][0].shape[0] // 2
    for k, grad in enumerate(pair(down_k[...], down_g[...])):
        step(3, (slice(k * size, (k + 1) * size), every), grad.T)
    send(3)
    arrive(4)
    vocab = states[4][0].shape[2]
    step(4, (0, every, every), embed_ref[:, 0:vocab] * scale)
    step(4, (1, every, every), head_ref[:, 0:vocab] * scale)
    send(4)
    arrive(1)
    size = states[1][0].shape[0] // 2
    cut = slice(3 * lanes, attn_k.shape[1])
    for k, grad in enumerate(pair(attn_k[:, cut], attn_g[:, cut])):
        step(1, (slice(k * size, (k + 1) * size), every), grad.T)
    send(1)
    arrive(5)
    step(5, (every, every), gain_ref[...] * scale)
    send(5)
    for i in range(6):
        for copy in copies(i):
            copy.wait()


def adam(scale, c_index, states, grads):
    shapes = []
    for group in states:
        shapes += [jax.ShapeDtypeStruct(group[0].shape, t) for t in (F32, F32, F32, BF)]
    args = [v for group in states for v in group] + list(grads)
    vmem, smem = pl.BlockSpec(memory_space=pltpu.VMEM), pl.BlockSpec(memory_space=pltpu.SMEM)
    hbm = pl.BlockSpec(memory_space=pl.ANY)
    return pl.pallas_call(
        adam_kernel,
        in_specs=[smem, smem] + [hbm] * 18 + [vmem] * len(grads),
        out_specs=[hbm] * len(shapes),
        out_shape=shapes,
        scratch_shapes=[pltpu.VMEM(s.shape, s.dtype) for s in shapes]
        + [pltpu.VMEM(v.shape, v.dtype) for v in args[:18]]
        + [pltpu.SemaphoreType.DMA((6, 4)), pltpu.SemaphoreType.DMA((6, 3))],
        compiler_params=pltpu.CompilerParams(vmem_limit_bytes=2 * VMEM_BYTES),
        cost_estimate=cheap(),
        name="adam",
    )(scale, c_index, *args)


def body(
    codes,
    doc_lengths,
    loss_mask,
    qkv_master,
    qkv_first,
    qkv_second,
    out_master,
    out_first,
    out_second,
    up_master,
    up_first,
    up_second,
    down_master,
    down_first,
    down_second,
    table_master,
    table_first,
    table_second,
    gain_master,
    gain_first,
    gain_second,
):
    place = Place()
    nz, ny, nb = place.nz, place.ny, len(place.blocks)
    c, z = place.c, place.z
    feat = qkv_master.shape[0]
    width = feat * place.dp
    total_rows = codes.shape[1]
    half_rows = total_rows // 2
    vocab = table_master.shape[1]
    thin = table_master.shape[2]

    joined = jnp.concatenate([codes, loss_mask, doc_lengths], 1)
    other = place.swap_c(joined)
    four = place.in_order(joined, other, 0)
    row = lax.dynamic_index_in_dim(four, z, 0, keepdims=False)
    codes_row = row[:total_rows]
    mask_row = row[total_rows : 2 * total_rows]
    lengths_row = row[2 * total_rows :]
    doc_ids, starts, local_pos = doc_layout(lengths_row, total_rows)
    targets = next_codes(codes_row, doc_ids, vocab - 1)
    first_row = c * half_rows
    my_codes = lax.dynamic_slice_in_dim(codes_row, first_row, half_rows, 0)
    my_local = lax.dynamic_slice_in_dim(local_pos, first_row, half_rows, 0)
    my_targets = lax.dynamic_slice_in_dim(targets, first_row, half_rows, 0)
    my_mask = lax.dynamic_slice_in_dim(mask_row, first_row, half_rows, 0).astype(F32)
    c_index = jnp.reshape(c, (1,)).astype(jnp.int32)
    starts_col = starts.reshape(total_rows, 1)

    def halves(matrix, axis):
        size = matrix.shape[axis] // 2
        keep = lax.dynamic_slice_in_dim(matrix, c * size, size, axis)
        send = lax.dynamic_slice_in_dim(matrix, (1 - c) * size, size, axis)
        return keep, send

    cols = -(-(vocab + 3) // 128) * 128
    table_t = jnp.swapaxes(table_master.astype(BF), 1, 2)
    embed_p = jnp.concatenate(
        [table_t[0], gain_master.astype(BF).T, jnp.zeros((thin, cols - vocab - 3), BF)], 1
    )
    head_p = jnp.concatenate([table_t[1], jnp.zeros((thin, cols - vocab), BF)], 1)
    slots = Slots()
    g_embed, g_head = GatherTable(place, embed_p), Gather(place, head_p, 0)

    qkv_b, out_b, up_b, down_b = (
        v.astype(BF) for v in (qkv_master, out_master, up_master, down_master)
    )
    qkv_k, qkv_s = (v.reshape(feat, -1) for v in halves(qkv_b, 2))
    out_k, out_s = (v.T for v in halves(out_b, 0))
    up_k, up_s = halves(up_b, 1)
    down_k, down_s = (v.T for v in halves(down_b, 0))
    units = [v.shape[1] for v in (qkv_k, out_k, up_k, down_k)]
    keep = jnp.concatenate([qkv_k, out_k, up_k, down_k], 1)
    send = jnp.concatenate([qkv_s, out_s, up_s, down_s], 1)
    recv = place.swap_c(send)
    chip = place.in_order(keep, recv, 0)
    edges = [sum(units[:i]) for i in range(5)]
    g_attn = Gather(place, chip[:, : edges[2]], 1, [(0, units[0]), (units[0], edges[2])])
    g_up = Gather(place, chip[:, edges[2] : edges[3]], 1)
    g_down = Gather(place, chip[:, edges[3] :], 1)

    block = jnp.asarray([k for k, _ in place.blocks], jnp.int32)
    block_x = jnp.asarray([k for _, k in place.blocks], jnp.int32)
    chip_at = ((place.y + block) % ny) * 2 + (place.x ^ block_x)
    feature = (
        chip_at[:, None] * (2 * feat) + jnp.arange(2 * feat, dtype=jnp.int32)[None, :]
    ).reshape(width)
    freqs = jnp.exp((feature // 2).astype(F32) * (-2.0 * math.log(10000.0) / width))
    local_c = Cell(my_local)
    fence(local_c, g_attn.wide)
    angles = local_c.v.astype(F32)[:, None] * freqs[None, :]
    coded = Cell(jnp.where((feature % 2 == 0)[None, :], jnp.sin(angles), jnp.cos(angles)))

    def branch(lefts, gather, span):
        theirs = back(lefts, gather, span, half_rows, half_rows, BF)
        got = place.swap_c(theirs)
        return back(lefts, gather, span, 0, half_rows, F32), got

    def table(gather):
        a, b = (jnp.stack(v) for v in gather.pieces())
        mine = jnp.concatenate([a, b], 1).reshape(nb, 1, nz * thin, cols)
        return place.in_order(mine, place.swap_c(mine), 1).reshape(width, cols)

    def code_rows(half):
        own = lax.dynamic_slice_in_dim(codes_row, half * half_rows, half_rows, 0)
        gain_codes = vocab + jnp.arange(16, dtype=jnp.int32)
        return jnp.concatenate([own, jnp.where(gain_codes < vocab + 3, gain_codes, -1)])[:, None]

    codes_c = cells(code_rows(c), code_rows(1 - c))
    g_embed.over_z()
    g_attn.over_z()
    fence(g_attn.parts, coded)
    slots.slot([g_attn.near, g_embed.around])
    g_up.over_z(g_attn.parts)
    g_down.over_z(g_up.parts)
    slots.slot([g_up.near, g_attn.far])
    g_head.over_z(g_down.parts)
    found, found_other = lookup(codes_c[0].v, codes_c[1].v, g_embed)
    start, attn_m, gains = start_norm(nb, c_index, found, place.swap_c(found_other), coded.v)
    gains = [gains[i : i + 1] for i in range(3)]
    one_hot = (my_codes[:, None] == jnp.arange(cols, dtype=jnp.int32)[None, :]).astype(BF)
    attn_c, other_c = cells(attn_m, place.swap_c(attn_m))

    slots.slot([g_down.near, g_up.far], attn_c, other_c, g_head.parts)
    span_qkv = (0, nz // 2 * units[0])
    span_out = (span_qkv[1], nz // 2 * edges[2])
    span_up, span_down = (0, nz // 2 * units[2]), (0, nz // 2 * units[3])
    attn_in, qkv, _ = across(attn_c.v, other_c.v, g_attn, span_qkv)
    mixed, lse = zip(*(attention(c_index, starts_col, v) for v in qkv))
    theirs_c = Cell(back(mixed, g_attn, span_out, half_rows, half_rows, BF))
    mine_c = Cell(back(mixed, g_attn, span_out, 0, half_rows, F32))

    slots.slot([g_head.near, g_down.far], theirs_c, mine_c)
    middle, ffn_m = norm([start, mine_c.v, place.swap_c(theirs_c.v)], gains[1])
    ffn_in, hidden, slope = across(ffn_m, place.swap_c(ffn_m), g_up, span_up, "gelu")
    hidden_c = cells(*hidden)
    slots.slot([g_head.far], *hidden_c)
    hidden = [v.v for v in hidden_c]
    final, features = norm([middle, *branch(hidden, g_down, span_down)], gains[2])
    a, b = (jnp.stack(v) for v in g_head.pieces())
    mine = jnp.concatenate([a, b], 1).reshape(nb, 1, nz * thin, cols)
    head_t = place.in_order(mine, place.swap_c(mine), 1).reshape(width, cols)
    logits = dot(features, head_t)
    logits = jnp.where(jnp.arange(cols)[None, :] < vocab, logits, -1e30)
    loss_local, grad_logits = head_loss(logits, my_targets, my_mask)

    slots = Slots()
    cut = 2 * feat

    def matrix_sum(*pairs):
        whole = weight_grads(place, *pairs)
        groups, start_at = [], 0
        for _, rights in pairs:
            size = rights[0].shape[1] // (nz // 2)
            groups.append((start_at, start_at + size))
            start_at += size
        return Reduce(place, whole, 1, groups)

    def table_sum(left, right, extra=None):
        def by_c(values):
            size = nz * thin
            even, odd = (
                jnp.concatenate([values[..., (2 * i + k) * size : (2 * i + k + 1) * size] for i in range(nb)], -1)
                for k in (0, 1)
            )
            return jnp.where(c == 0, even, odd), jnp.where(c == 0, odd, even)

        left_k, left_s = by_c(left)
        own = dot(left_k, right, TN)
        sent = dot(left_s, right, TN)
        if extra is not None:
            extra_k, extra_s = (
                jnp.pad(v.T, ((0, 0), (vocab, cols - vocab - extra.shape[0]))) for v in by_c(extra)
            )
            own, sent = own + extra_k, sent + extra_s
        got = place.swap_c(sent.astype(BF))
        chip_sum = (own + got.astype(F32)).astype(BF).reshape(nb, 2, nz // 2 * thin, cols)
        return Reduce(place, [chip_sum[:, 0], chip_sum[:, 1]], 0)

    r_head = table_sum(features, grad_logits)
    grad_feat = dot(grad_logits, head_t, NT)
    grad_final, grad_down, gain_three = norm_back([grad_feat], [], final, gains[2])
    grad_down_c, other_c = cells(grad_down, place.swap_c(grad_down))
    slots.slot([r_head.near], grad_down_c, other_c)
    grad_down, other = grad_down_c.v, other_c.v
    r_down = matrix_sum((jnp.concatenate([grad_down, other], 0), hidden))

    grad_down_c, other_c = cells(grad_down, other)
    slots.slot([r_down.near, r_head.far], grad_down_c, other_c)
    _, grad_up, _ = across(grad_down_c.v, other_c.v, g_down, span_down, "slope", slope)
    theirs_c = Cell(back(grad_up, g_up, span_up, half_rows, half_rows, BF))
    mine_c = Cell(back(grad_up, g_up, span_up, 0, half_rows, F32))
    r_up = matrix_sum((ffn_in, grad_up))

    slots.slot([r_up.near, r_down.far], theirs_c, mine_c)
    grad_mid, grad_out, gain_two = norm_back(
        [mine_c.v, place.swap_c(theirs_c.v)], [grad_final], middle, gains[1]
    )
    grad_out, grad_mixed, _ = across(grad_out, place.swap_c(grad_out), g_attn, span_out)
    grad_qkv = [
        attention_back(c_index, starts_col, q, o, g, ls)
        for q, o, g, ls in zip(qkv, mixed, grad_mixed, lse)
    ]
    r_attn = matrix_sum((attn_in, grad_qkv), (grad_out, mixed))
    grad_qkv_c = cells(*grad_qkv)
    theirs_c = Cell(back(grad_qkv, g_attn, span_qkv, half_rows, half_rows, BF))

    slots.slot([r_attn.near, r_up.far], theirs_c, *grad_qkv_c)
    mine_c = Cell(back([v.v for v in grad_qkv_c], g_attn, span_qkv, 0, half_rows, F32))
    r_down.over_z()
    grad_start, _, gain_one = norm_back(
        [mine_c.v, place.swap_c(theirs_c.v)], [grad_mid], start, gains[0]
    )
    gain_grad = jnp.concatenate([gain_one, gain_two, gain_three], 0)
    r_embed = table_sum((grad_start * math.sqrt(width)).astype(BF), one_hot, gain_grad)

    slots.slot([r_attn.far, r_embed.near])
    r_up.over_z(r_down.got)
    slots.slot([r_embed.far])
    r_head.over_z(slots.flight[0])
    r_attn.over_z(r_up.got)
    r_embed.over_z(r_up.got)

    def shards(total):
        keep_g, send_g = halves(total, 0)
        return keep_g, place.swap_c(send_g)

    head_sum, down_sum, up_sum = r_head.result(), r_down.result(), r_up.result()
    down_k, down_g = shards(down_sum)
    up_k, up_g = shards(up_sum)
    attn_sum = r_attn.result()
    attn_k, attn_g = shards(attn_sum)
    embed_sum = r_embed.result()
    squares = sum(
        jnp.sum(v * v) for v in (head_sum, down_sum, up_sum, attn_sum, embed_sum)
    )
    stats = jnp.stack([loss_local, jnp.sum(my_mask), squares])
    stats = place.total(stats)
    loss_all, count_all = stats[0], stats[1]
    norm_all = jnp.sqrt(stats[2] / (count_all * count_all))
    factor = jnp.minimum(1.0, CLIP_NORM / (norm_all + 1e-06))
    scale = jnp.reshape(factor / count_all, (1,))
    states = (
        [jnp.swapaxes(v, 0, 1) for v in (qkv_master, qkv_first, qkv_second)],
        (out_master, out_first, out_second),
        (up_master, up_first, up_second),
        (down_master, down_first, down_second),
        [jnp.swapaxes(v, 1, 2) for v in (table_master, table_first, table_second)],
        (gain_master, gain_first, gain_second),
    )
    gain_sum = embed_sum[:, vocab : vocab + 3].T
    grads = (attn_k, attn_g, up_k, up_g, down_k, down_g, embed_sum, head_sum, gain_sum)
    new = list(adam(scale, c_index, states, grads))
    new[0:4] = [jnp.swapaxes(v, 0, 1) for v in new[0:4]]
    new[16:20] = [jnp.swapaxes(v, 1, 2) for v in new[16:20]]
    return tuple(new) + (loss_all, count_all, norm_all)


def solution(mesh):
    rows, cols = P("dp", None, "tensor"), P("tensor", "dp")
    plain, both, gain = P("dp", "tensor"), P(None, None, ("dp", "tensor")), P(None, ("dp", "tensor"))
    kinds = (rows, cols, plain, cols, both, gain)
    in_specs = (P("dp", None),) * 3 + tuple(k for k in kinds for _ in range(3))
    out_specs = tuple(k for k in kinds for _ in range(4)) + (P(),) * 3
    return jax.shard_map(body, mesh=mesh, in_specs=in_specs, out_specs=out_specs, check_vma=False)
```
